256 devices in a mesh: dp: 16 (over x, z_hi, core), seq: 16 (over y, z_lo).
Axes of the slice: x: 4, y: 4, z: 8 (z_hi: 2, z_lo: 4; z = z_hi * 4 + z_lo), core: 2. Of those that a mesh axis runs over, the one named last changes fastest.
Arguments:
- tokens: bfloat16 [16, 2048, 1536], P('dp', 'seq'), may hold values from -8 to 8
- lengths: int32 [16], P('dp'), may hold values from 512 to 2048
- cotangent: bfloat16 [16, 2048, 1536], P('dp', 'seq'), may hold values from -6 to 6
- gain: float32 [1536], replicated, may hold values from 0.25 to 1.75
- w_q: bfloat16 [1536, 512], replicated, may hold values from -1 to 1
- w_kv: bfloat16 [1536, 320], replicated, may hold values from -1 to 1
- w_o: bfloat16 [768, 1536], replicated, may hold values from -0.21875 to 0.21875
Outputs:
- grad_tokens: bfloat16 [16, 2048, 1536], P('dp', 'seq')
- grad_wq: float32 [1536, 512], P(('dp', 'seq'))
- grad_wkv: float32 [1536, 320], P(('dp', 'seq'))
- grad_wo_t: float32 [1536, 768], P(('dp', 'seq'))
The draws below stay inside these ranges and needn't reach their ends.
All inputs are finite; a program needn't handle non-finite values.
Results may differ from the reference program's by a relative error of at most 0.034.
Values may be sent and summed in bfloat16 or wider, within the bound.
A program may use at most 128 MiB of HBM per device.

```python
import jax
import jax.numpy as jnp
from jax import lax

D = 1536
HEADS = 4
HK = 128
HV = 192
KEYS = 2048
EXAMPLES = 16


def draw_tokens(key, part):
    key = jax.random.fold_in(key, 3)
    noise_key = jax.random.fold_in(key, 0)
    base = jnp.clip(jax.random.normal(noise_key, (EXAMPLES, KEYS, D), jnp.float32), -6.0, 6.0)
    return base.astype(jnp.bfloat16)


def draw_w_q(key, part):
    key = jax.random.fold_in(key, 5)
    weights = jnp.clip(jax.random.normal(key, (D, HEADS * HK), jnp.float32), -6.0, 6.0) * D ** (-0.5)
    return weights.astype(jnp.bfloat16)


def draw_w_kv(key, part):
    key = jax.random.fold_in(key, 7)
    weights = jnp.clip(jax.random.normal(key, (D, HK + HV), jnp.float32), -6.0, 6.0) * D ** (-0.5)
    return weights.astype(jnp.bfloat16)


def touch_ends(entries, key, low, largest):
    place = [jax.random.randint(jax.random.fold_in(key, axis), (), 0, length) for axis, length in enumerate(entries.shape)]
    main_axis = entries.shape.index(max(entries.shape))
    neighbour = place[:main_axis] + [(place[main_axis] + 1) % entries.shape[main_axis]] + place[main_axis + 1:]
    return entries.at[tuple(place)].set(low).at[tuple(neighbour)].set(largest)


def level_of(rng, dims, pieces, least, high):
    level = 1.0
    for axis_at, blocks in pieces:
        draws = jax.random.uniform(jax.random.fold_in(jax.random.fold_in(rng, 6), axis_at), (blocks,), jnp.float32, least / len(pieces), high / len(pieces))
        level = level * jnp.repeat(jnp.exp(draws), dims[axis_at] // blocks).reshape((-1,) + (1,) * (len(dims) - 1 - axis_at))
    return level


def normal_values(stream_key, dims, scale, bound, cuts=(), kind=jnp.bfloat16):
    factor_of = level_of(stream_key, dims, cuts, -0.22, 0.18) if cuts else 1.0
    entries = jax.random.normal(stream_key, dims, jnp.float32) * scale * factor_of
    return jnp.minimum(jnp.maximum(entries, -bound), bound).astype(kind)


def setup_inputs(seed: int = 0) -> dict:
    arg_keys = jax.random.split(jax.random.key(seed), 8)
    return {
        "tokens": draw_tokens(jax.random.fold_in(arg_keys[7], 71), 0),
        "lengths": touch_ends(jax.random.randint(arg_keys[1], (EXAMPLES,), KEYS // 4, KEYS + 1), jax.random.fold_in(arg_keys[1], 1), KEYS // 4, KEYS).astype(jnp.int32),
        "cotangent": normal_values(arg_keys[2], (EXAMPLES, KEYS, D), 1.0, 6.0, ((0, 16), (1, 16))),
        "gain": jnp.clip(1.0 + 0.15 * jax.random.normal(arg_keys[3], (D,), jnp.float32), 0.25, 1.75),
        "w_q": draw_w_q(jax.random.fold_in(arg_keys[7], 71), 0),
        "w_kv": draw_w_kv(jax.random.fold_in(arg_keys[7], 71), 0),
        "w_o": normal_values(arg_keys[6], (HEADS * HV, D), (HEADS * HV) ** -0.5, 0.21875),
    }


EPS = 1e-06

def reference(tokens, lengths, cotangent, gain, w_q, w_kv, w_o):
    scale = HK ** (-0.5)

    def one(carry, item):
        x, g, length = item
        xf = x.astype(jnp.float32)
        rscale = lax.rsqrt(lax.optimization_barrier(jnp.mean(xf * xf, axis=-1, keepdims=True)) + EPS)
        normed = (xf * rscale * gain).astype(jnp.bfloat16)
        query = jnp.dot(normed, w_q, preferred_element_type=jnp.float32).astype(jnp.bfloat16)
        keyval = jnp.dot(normed, w_kv, preferred_element_type=jnp.float32).astype(jnp.bfloat16)
        keys = keyval[:, :HK]
        vals = keyval[:, HK:]
        valid = jnp.arange(KEYS, dtype=jnp.int32)[None, :] < length
        d_att = jnp.dot(g, w_o.T, preferred_element_type=jnp.float32).astype(jnp.bfloat16)
        outs = []
        dqs = []
        d_key = jnp.zeros((KEYS, HK), jnp.float32)
        d_val = jnp.zeros((KEYS, HV), jnp.float32)
        for head in range(HEADS):
            q_head = query[:, head * HK:(head + 1) * HK]
            da_head = d_att[:, head * HV:(head + 1) * HV]
            scores = jnp.dot(q_head, keys.T, preferred_element_type=jnp.float32) * scale
            scores = jnp.where(valid, scores, -1e+30)
            top = lax.optimization_barrier(jnp.max(scores, axis=-1, keepdims=True))
            expo = jnp.exp(scores - top)
            prob = expo / lax.optimization_barrier(jnp.sum(expo, axis=-1, keepdims=True))
            prob_b = prob.astype(jnp.bfloat16)
            att = jnp.dot(prob_b, vals, preferred_element_type=jnp.float32).astype(jnp.bfloat16)
            delta = lax.optimization_barrier(jnp.sum(da_head.astype(jnp.float32) * att.astype(jnp.float32), axis=-1, keepdims=True))
            dpv = jnp.dot(da_head, vals.T, preferred_element_type=jnp.float32)
            d_score = (prob * (dpv - delta) * scale).astype(jnp.bfloat16)
            dqs.append(jnp.dot(d_score, keys, preferred_element_type=jnp.float32).astype(jnp.bfloat16))
            d_key = d_key + jnp.dot(d_score.T, q_head, preferred_element_type=jnp.float32)
            d_val = d_val + jnp.dot(prob_b.T, da_head, preferred_element_type=jnp.float32)
            outs.append(att)
        attended = jnp.concatenate(outs, axis=1)
        d_query = jnp.concatenate(dqs, axis=1)
        d_keyval = jnp.concatenate([d_key, d_val], axis=1).astype(jnp.bfloat16)
        gq = carry[0] + jnp.dot(normed.T, d_query, preferred_element_type=jnp.float32)
        gkv = carry[1] + jnp.dot(normed.T, d_keyval, preferred_element_type=jnp.float32)
        gwo = carry[2] + jnp.dot(g.T, attended, preferred_element_type=jnp.float32)
        d_normed = jnp.dot(d_query, w_q.T, preferred_element_type=jnp.float32) + jnp.dot(d_keyval, w_kv.T, preferred_element_type=jnp.float32)
        inner = lax.optimization_barrier(jnp.mean(xf * gain * d_normed, axis=-1, keepdims=True))
        grad_x = g.astype(jnp.float32) + rscale * gain * d_normed - xf * rscale ** 3 * inner
        return ((gq, gkv, gwo), grad_x.astype(jnp.bfloat16))
    init = (jnp.zeros((D, HEADS * HK), jnp.float32), jnp.zeros((D, HK + HV), jnp.float32), jnp.zeros((D, HEADS * HV), jnp.float32))
    grads, grad_tokens = lax.scan(one, init, (tokens, cotangent, lengths.astype(jnp.int32)))
    return (grad_tokens, grads[0], grads[1], grads[2])
```

```python
import functools

import jax
import jax.numpy as jnp
from jax import lax
from jax.experimental import pallas as pl
from jax.experimental.pallas import tpu as pltpu
from jax.sharding import PartitionSpec as P

EPS = 1e-06
HK = 128
HV = 192
HEADS = 4
KV = HK + HV
D = 1536
ROWS = 128
ALL = HEADS * ROWS
CHUNK = 512
LOG2E = 1.4426950408889634
SCALE = HK ** (-0.5)
F32 = jnp.float32
BF16 = jnp.bfloat16
NT = (((1,), (1,)), ((), ()))
NN = (((1,), (0,)), ((), ()))

COLS = (HEADS * HV, HEADS * HK, KV)


def mm(a, b, dims=NN):
    return lax.dot_general(a, b, dims, preferred_element_type=F32)


def make_slots():
    names = []
    names += [("agz", d) for d in (1, 2, 3)]
    names += [("agy", j, d) for j in (1, 3) for d in range(4)]
    names += [("agr", d) for d in range(4)]
    names += [("sib", k) for k in ("n", "c", "a", "q", "kv")]
    names += [("rs1", j, s) for j in (1, 3) for s in ("opp", "own")]
    names += [("rs2", j) for j in (1, 3)]
    names += [("rsz", d) for d in (1, 2, 3)]
    for w in range(3):
        names += [("wx1", w, h) for h in (0, 1)]
        names += [("wx2", w, h) for h in (0, 1)]
        names += [("wy", w, j) for j in (1, 2, 3)]
        names += [("wz", w, a, b) for a in (0, 1) for b in range(4) if a or b]
    return {name: i for i, name in enumerate(names)}


SLOT = make_slots()


def kernel(
    len_ref, tok_ref, cot_ref, gain_ref, wq_ref, wkv_ref, wo_ref,
    gtok_ref, gwq_ref, gwkv_ref, gwo_ref,
    kvt, vals, scores, probs, ub, qt, qts, dat, dats, normed, rscale, dn,
    t, r1a, r1b, fa, fb, r2a, r2b, zsend, rz,
    nall, call, n2, c2, a2, dq2, dkv2,
    p0, p1, p2, rx0, rx1, rx2, fx0, fx1, fx2, sx0, sx1, sx2,
    y0, y1, y2, ry0, ry1, ry2, ys0, ys1, ys2, z0, z1, z2, rz0, rz1, rz2,
    ssem, rsem,
):
    dp, seq = lax.axis_index("dp"), lax.axis_index("seq")
    x, zh, c = dp // 4, (dp // 2) % 2, dp % 2
    y, zl = seq // 4, seq % 4
    xs = (x, x + 1 - 2 * (x % 2), (x + 2) % 4, 3 - x)
    ys = (y, y + 1 - 2 * (y % 2), (y + 2) % 4, 3 - y)
    other = 1 - c

    def dev(x_=x, zh_=zh, c_=c, y_=y, zl_=zl):
        return (x_ * 4 + zh_ * 2 + c_, y_ * 4 + zl_)

    sent = []

    def send(name, src, dst, to):
        i = SLOT[name]
        copy = pltpu.make_async_remote_copy(
            src_ref=src, dst_ref=dst, send_sem=ssem.at[i], recv_sem=rsem.at[i],
            device_id=to, device_id_type=pl.DeviceIdType.MESH,
        )
        copy.start()
        sent.append(copy)
        return copy

    peers = [dev(c_=other), dev(x_=xs[1]), dev(x_=xs[3])]
    peers += [dev(y_=ys[j]) for j in (1, 2, 3)]
    peers += [
        dev(zh_=(zh + a) % 2, zl_=(zl + b) % 4) for a in (0, 1) for b in range(4) if a or b
    ]
    barrier = pltpu.get_barrier_semaphore()
    for peer in peers:
        pl.semaphore_signal(barrier, inc=1, device_id=peer, device_id_type=pl.DeviceIdType.MESH)

    xf = tok_ref[...].astype(F32)
    rs = lax.rsqrt(jnp.mean(xf * xf, axis=-1, keepdims=True) + EPS)
    rscale[...] = rs
    nf = xf * rs * gain_ref[...]
    nb = nf.astype(BF16)
    normed[...] = nb
    kv = mm(nb, wkv_ref[...])
    kvt[0, :, 0:ROWS] = kv.T.astype(BF16)
    pl.semaphore_wait(barrier, len(peers))

    agz, agy, agr = {}, {}, {}
    lane = [slice(ROWS * d, ROWS * (d + 1)) for d in range(4)]

    def to_y(d):
        for j in (1, 3):
            agy[j, d] = send(("agy", j, d), kvt.at[0, :, lane[d]], kvt.at[j, :, lane[d]], dev(y_=ys[j]))

    for d in (1, 3, 2):
        agz[d] = send(("agz", d), kvt.at[0, :, lane[0]], kvt.at[0, :, lane[d]], dev(zl_=(zl + 4 - d) % 4))
    to_y(0)

    q = mm(normed[...], wq_ref[...])
    for h in range(HEADS):
        qt[:, lane[h]] = q[:, lane[h]].T.astype(BF16)
    for d in (1, 3):
        agz[d].wait_recv()
        to_y(d)
    for h in range(HEADS):
        da = mm(wo_ref[HV * h : HV * (h + 1), :], cot_ref[...], NT)
        dat[:, lane[h]] = da.astype(BF16)
    agz[2].wait_recv()
    to_y(2)

    nall[...] = normed[...].T.reshape(4, 2, 2, 96, ROWS)
    sib = dev(c_=other)
    sib_n = send(("sib", "n"), nall.at[:, :, other], n2.at[:, :, :, ROWS : 2 * ROWS], sib)
    n2[:, :, :, 0:ROWS] = nall[:, :, c]
    call[...] = cot_ref[...].T.reshape(4, 2, 2, 96, ROWS)
    sib_c = send(("sib", "c"), call.at[:, :, other], c2.at[:, :, :, ROWS : 2 * ROWS], sib)
    c2[:, :, :, 0:ROWS] = call[:, :, c]

    length = len_ref[0]
    tops = [None]

    def score(j, d):
        first = (ys[j] * 4 + (zl + d) % 4) * ROWS
        blk = kvt[j, :, lane[d]]
        k = blk[0:HK, :].T
        vals[j, lane[d], :] = blk[HK:KV, :].T
        s = mm(k, qt[...]) * (SCALE * LOG2E)
        pos = first + lax.broadcasted_iota(jnp.int32, (ROWS, ALL), 0)
        s = jnp.where(pos < length, s, -1e30)
        scores[j, lane[d], :] = s
        part = jnp.max(s.reshape(ROWS // 8, 8, ALL), axis=0)
        tops[0] = part if tops[0] is None else jnp.maximum(tops[0], part)

    for d in range(4):
        score(0, d)
    relay = {}
    for d, j, to in ((0, 1, 3), (2, 3, 1), (1, 1, 3), (3, 3, 1)):
        agy[j, d].wait_recv()
        relay[d] = send(("agr", d), kvt.at[j, :, lane[d]], kvt.at[2, :, lane[d]], dev(y_=ys[to]))
        score(j, d)
    for j, d in ((1, 2), (1, 3), (3, 0), (3, 1)):
        agy[j, d].wait_recv()
        score(j, d)
    for d in (0, 2, 1, 3):
        relay[d].wait_recv()
        score(2, d)

    top = jnp.max(tops[0], axis=0, keepdims=True)
    total = jnp.zeros((8, ALL), F32)
    att = jnp.zeros((HV, ALL), F32)
    for j in range(4):
        for d in range(4):
            e = jnp.exp2(scores[j, lane[d], :] - top)
            total = total + jnp.sum(e.reshape(ROWS // 8, 8, ALL), axis=0)
            probs[j, lane[d], :] = e.astype(BF16)
        att = att + mm(kvt[j, HK:KV, :], probs[j])
    inv = 1.0 / jnp.sum(total, axis=0, keepdims=True)
    att_b = (att * inv).astype(BF16)
    da = dat[...].astype(F32)
    delta = jnp.sum(da * att_b.astype(F32), axis=0, keepdims=True)
    dats[...] = (da * inv).astype(BF16)
    qts[...] = (qt[...].astype(F32) * (inv * SCALE)).astype(BF16)
    for h in range(HEADS):
        a2[HV * h : HV * (h + 1), 0:ROWS] = att_b[:, lane[h]]
    mine, theirs = slice(0, ROWS), slice(ROWS, 2 * ROWS)
    sib_a = send(("sib", "a"), a2.at[:, mine], a2.at[:, theirs], sib)

    def backward(j, dq):
        for d in range(4):
            dpv = mm(vals[j, lane[d], :], dat[...])
            u = probs[j, lane[d], :].astype(F32) * (dpv - delta)
            ub[j, lane[d], :] = u.astype(BF16)
        dq = dq + mm(kvt[j, 0:HK, :], ub[j])
        t[j, 0:HK, :] = mm(qts[...], ub[j], NT).astype(BF16)
        t[j, HK:KV, :] = mm(dats[...], probs[j], NT).astype(BF16)
        return dq

    alpha, beta = slice(0, 256), slice(256, 512)
    to1, to3 = dev(y_=ys[1]), dev(y_=ys[3])
    rs1 = {}
    dq = backward(2, jnp.zeros((HK, ALL), F32))
    rs1[1, "opp"] = send(("rs1", 1, "opp"), t.at[2, :, alpha], r1a.at[1], to1)
    rs1[3, "opp"] = send(("rs1", 3, "opp"), t.at[2, :, beta], r1b.at[1], to3)
    dq = backward(1, dq)
    rs1[1, "own"] = send(("rs1", 1, "own"), t.at[1, :, alpha], r1a.at[0], to1)
    dq = backward(3, dq)
    rs1[3, "own"] = send(("rs1", 3, "own"), t.at[3, :, beta], r1b.at[0], to3)

    part, rx, fx, sx = (p0, p1, p2), (rx0, rx1, rx2), (fx0, fx1, fx2), (sx0, sx1, sx2)
    yb, ry, ysum = (y0, y1, y2), (ry0, ry1, ry2), (ys0, ys1, ys2)
    zb, rzb = (z0, z1, z2), (rz0, rz1, rz2)
    grads = (gwo_ref, gwq_ref, gwkv_ref)
    x1, x3 = dev(x_=xs[1]), dev(x_=xs[3])
    wx1, wx2, wy, wz = {}, {}, {}, {}

    def w_part(w, rows, right):
        for i in (2, 1, 3, 0):
            left = rows[xs[i]].reshape(192, 2 * ROWS)
            part[w][i] = mm(left, right[...], NT).reshape(2, 96, COLS[w]).astype(BF16)
            if i == 1:
                wx1[w, 0] = send(("wx1", w, 0), part[w].at[1:3, 0], rx[w].at[0], x1)
            if i == 3:
                wx1[w, 1] = send(("wx1", w, 1), part[w].at[2:4, 1], rx[w].at[1], x3)

    def w_x2(w):
        wx1[w, 0].wait_recv()
        fx[w][0] = (part[w][3, 0].astype(F32) + rx[w][0, 1].astype(F32)).astype(BF16)
        wx2[w, 0] = send(("wx2", w, 0), fx[w].at[0], sx[w].at[0], x3)
        wx1[w, 1].wait_recv()
        fx[w][1] = (part[w][1, 1].astype(F32) + rx[w][1, 0].astype(F32)).astype(BF16)
        wx2[w, 1] = send(("wx2", w, 1), fx[w].at[1], sx[w].at[1], x1)

    def w_y(w):
        sums = []
        for h in (0, 1):
            wx2[w, h].wait_recv()
            sums.append(
                part[w][0, h].astype(F32) + rx[w][h, h].astype(F32) + sx[w][h].astype(F32)
            )
        for k in range(4):
            rows = slice(24 * k, 24 * (k + 1))
            yb[w][k] = jnp.concatenate([sums[0][rows], sums[1][rows]], axis=0).astype(BF16)
        for j in (2, 1, 3):
            wy[w, j] = send(("wy", w, j), yb[w].at[ys[j]], ry[w].at[j - 1], dev(y_=ys[j]))

    def w_z(w):
        total = yb[w][y].astype(F32)
        for j in (1, 3, 2):
            wy[w, j].wait_recv()
            total = total + ry[w][j - 1].astype(F32)
        ysum[w][...] = total
        zb[w][...] = jnp.zeros_like(zb[w])
        for k in range(8):
            zb[w][k, 0:6, :] = ysum[w][6 * k : 6 * (k + 1), :]
        for a, b in ((1, 0), (1, 1), (1, 3), (1, 2), (0, 2), (0, 1), (0, 3)):
            zh_, zl_ = (zh + a) % 2, (zl + b) % 4
            wz[w, a, b] = send(
                ("wz", w, a, b), zb[w].at[zh_ * 4 + zl_], rzb[w].at[a * 4 + b - 1], dev(zh_=zh_, zl_=zl_)
            )

    def w_end(w):
        total = zb[w][zh * 4 + zl]
        for a, b in ((0, 1), (0, 3), (0, 2), (1, 0), (1, 1), (1, 3), (1, 2)):
            wz[w, a, b].wait_recv()
            total = total + rzb[w][a * 4 + b - 1]
        grads[w][...] = total[0:6, :]

    sib_c.wait_recv()
    sib_a.wait_recv()
    w_part(0, c2, a2)

    dq = backward(0, dq)
    dq_b = (dq * (inv * SCALE)).astype(BF16)
    for h in range(HEADS):
        dq2[HK * h : HK * (h + 1), mine] = dq_b[:, lane[h]]
    sib_q = send(("sib", "q"), dq2.at[:, mine], dq2.at[:, theirs], sib)

    rs1[1, "opp"].wait_recv()
    fa[...] = (t[3, :, alpha].astype(F32) + r1a[1].astype(F32)).astype(BF16)
    rs2a = send(("rs2", 3), fa, r2a, to3)
    rs1[3, "opp"].wait_recv()
    fb[...] = (t[1, :, beta].astype(F32) + r1b[1].astype(F32)).astype(BF16)
    rs2b = send(("rs2", 1), fb, r2b, to1)

    sib_n.wait_recv()
    sib_q.wait_recv()
    w_part(1, n2, dq2)
    w_x2(0)

    rs1[1, "own"].wait_recv()
    rs2a.wait_recv()
    sum_a = t[0, :, alpha].astype(F32) + r1a[0].astype(F32) + r2a[...].astype(F32)
    zsend[:, alpha] = sum_a.astype(BF16)
    rsz = {}
    rsz[1] = send(("rsz", 1), zsend.at[:, lane[1]], rz.at[0], dev(zl_=(zl + 1) % 4))
    rs1[3, "own"].wait_recv()
    rs2b.wait_recv()
    sum_b = t[0, :, beta].astype(F32) + r1b[0].astype(F32) + r2b[...].astype(F32)
    zsend[:, beta] = sum_b.astype(BF16)
    for d in (2, 3):
        rsz[d] = send(("rsz", d), zsend.at[:, lane[d]], rz.at[d - 1], dev(zl_=(zl + d) % 4))

    w_x2(1)
    dqn = jnp.concatenate([dq2[HK * h : HK * (h + 1), mine].T for h in range(HEADS)], axis=1)
    dn[...] = mm(dqn, wq_ref[...], NT)
    w_y(0)

    dkv = zsend[:, lane[0]].astype(F32)
    for d in (1, 2, 3):
        rsz[d].wait_recv()
        dkv = dkv + rz[d - 1].astype(F32)
    dkv_b = dkv.astype(BF16)
    dkv2[:, mine] = dkv_b
    sib_kv = send(("sib", "kv"), dkv2.at[:, mine], dkv2.at[:, theirs], sib)
    dkvn = jnp.concatenate([dkv_b[0:HK].T, dkv_b[HK:KV].T], axis=1)
    sib_kv.wait_recv()
    w_part(2, n2, dkv2)

    w_y(1)
    d_normed = dn[...] + mm(dkvn, wkv_ref[...], NT)
    w_x2(2)
    w_z(0)
    xf = tok_ref[...].astype(F32)
    rs = rscale[...]
    gd = gain_ref[...] * d_normed
    inner = jnp.mean(xf * gd, axis=-1, keepdims=True)
    out = cot_ref[...].astype(F32) + rs * gd - xf * (rs * rs * rs * inner)
    gtok_ref[...] = out.astype(BF16)
    w_y(2)
    w_z(1)
    w_z(2)
    for w in range(3):
        w_end(w)
    for copy in sent:
        copy.wait_send()


def body(tokens, lengths, cotangent, gain, w_q, w_kv, w_o):
    vmem = pl.BlockSpec(memory_space=pltpu.VMEM)
    smem = pl.BlockSpec(memory_space=pltpu.SMEM)

    def per_weight(shape, kind):
        return [pltpu.VMEM(shape(n), kind) for n in COLS]

    scratch = [
        pltpu.VMEM((4, KV, CHUNK), BF16),
        pltpu.VMEM((4, CHUNK, HV), BF16),
        pltpu.VMEM((4, CHUNK, ALL), F32),
        pltpu.VMEM((4, CHUNK, ALL), BF16),
        pltpu.VMEM((4, CHUNK, ALL), BF16),
        pltpu.VMEM((HK, ALL), BF16),
        pltpu.VMEM((HK, ALL), BF16),
        pltpu.VMEM((HV, ALL), BF16),
        pltpu.VMEM((HV, ALL), BF16),
        pltpu.VMEM((ROWS, D), BF16),
        pltpu.VMEM((ROWS, 1), F32),
        pltpu.VMEM((ROWS, D), F32),
        pltpu.VMEM((4, KV, CHUNK), BF16),
        pltpu.VMEM((2, KV, 256), BF16),
        pltpu.VMEM((2, KV, 256), BF16),
        pltpu.VMEM((KV, 256), BF16),
        pltpu.VMEM((KV, 256), BF16),
        pltpu.VMEM((KV, 256), BF16),
        pltpu.VMEM((KV, 256), BF16),
        pltpu.VMEM((KV, CHUNK), BF16),
        pltpu.VMEM((3, KV, ROWS), BF16),
        pltpu.VMEM((4, 2, 2, 96, ROWS), BF16),
        pltpu.VMEM((4, 2, 2, 96, ROWS), BF16),
        pltpu.VMEM((4, 2, 96, 2 * ROWS), BF16),
        pltpu.VMEM((4, 2, 96, 2 * ROWS), BF16),
        pltpu.VMEM((COLS[0], 2 * ROWS), BF16),
        pltpu.VMEM((COLS[1], 2 * ROWS), BF16),
        pltpu.VMEM((COLS[2], 2 * ROWS), BF16),
    ]
    scratch += per_weight(lambda n: (4, 2, 96, n), BF16)
    scratch += per_weight(lambda n: (2, 2, 96, n), BF16)
    scratch += per_weight(lambda n: (2, 96, n), BF16)
    scratch += per_weight(lambda n: (2, 96, n), BF16)
    scratch += per_weight(lambda n: (4, 48, n), BF16)
    scratch += per_weight(lambda n: (3, 48, n), BF16)
    scratch += per_weight(lambda n: (48, n), F32)
    scratch += per_weight(lambda n: (8, 8, n), F32)
    scratch += per_weight(lambda n: (7, 8, n), F32)
    scratch += [pltpu.SemaphoreType.DMA((len(SLOT),)), pltpu.SemaphoreType.DMA((len(SLOT),))]
    grad_x, grad_wq, grad_wkv, grad_wo_t = pl.pallas_call(
        kernel,
        out_shape=(
            jax.ShapeDtypeStruct((ROWS, D), BF16),
            jax.ShapeDtypeStruct((6, COLS[1]), F32),
            jax.ShapeDtypeStruct((6, COLS[2]), F32),
            jax.ShapeDtypeStruct((6, COLS[0]), F32),
        ),
        in_specs=[smem] + [vmem] * 6,
        out_specs=(vmem,) * 4,
        scratch_shapes=scratch,
        compiler_params=pltpu.CompilerParams(
            collective_id=0, has_side_effects=True, vmem_limit_bytes=56 * 1024 * 1024
        ),
    )(lengths, tokens[0], cotangent[0], gain[None, :], w_q, w_kv, w_o)
    return grad_x[None], grad_wq, grad_wkv, grad_wo_t


def solution(mesh):
    return jax.shard_map(
        body,
        mesh=mesh,
        in_specs=(P("dp", "seq", None), P("dp"), P("dp", "seq", None), P(), P(), P(), P()),
        out_specs=(
            P("dp", "seq", None),
            P(("dp", "seq"), None),
            P(("dp", "seq"), None),
            P(("dp", "seq"), None),
        ),
        check_vma=False,
    )
```

```python
import functools

import jax
import jax.numpy as jnp
from jax import lax
from jax.experimental import pallas as pl
from jax.experimental.pallas import tpu as pltpu
from jax.sharding import PartitionSpec as P

EPS = 1e-06
HK = 128
HV = 192
HEADS = 4
KV = HK + HV
D = 1536
ROWS = 128
ALL = HEADS * ROWS
CHUNK = 512
LOG2E = 1.4426950408889634
SCALE = HK ** (-0.5)
F32 = jnp.float32
BF16 = jnp.bfloat16
NT = (((1,), (1,)), ((), ()))
NN = (((1,), (0,)), ((), ()))

COLS = (HEADS * HV, HEADS * HK, KV)


def mm(a, b, dims=NN):
    return lax.dot_general(a, b, dims, preferred_element_type=F32)


def make_slots():
    names = []
    names += [("agz", d) for d in (1, 2, 3)]
    names += [("agy", j, d) for j in (1, 3) for d in range(4)]
    names += [("agr", d) for d in range(4)]
    names += [("sib", k) for k in ("n", "c", "a", "q", "kv")]
    names += [("rs1", d, k) for d in range(4) for k in (0, 1)]
    names += [("rs2", d) for d in range(4)]
    names += [("rsz", d) for d in (1, 2, 3)]
    for w in range(2):
        names += [("wx1", w, h) for h in (0, 1)]
        names += [("wx2", w, h) for h in (0, 1)]
        names += [("wy", w, j) for j in (1, 2, 3)]
    names += [("wxy", i, j) for i in range(4) for j in range(4) if i or j]
    for w in range(3):
        names += [("wz", w, a, b) for a in (0, 1) for b in range(4) if a or b]
    return {name: i for i, name in enumerate(names)}


SLOT = make_slots()


def kernel(
    len_hbm, tok_hbm, cot_hbm, gain_hbm, wq_hbm, wkv_hbm, wo_hbm,
    gtok_hbm, gwq_hbm, gwkv_hbm, gwo_hbm,
    len_ref, tok_ref, cot_ref, gain_ref, wq_ref, wkv_ref, wo_ref,
    gtok_ref, gwq_ref, gwkv_ref, gwo_ref,
    kvt, vals, scores, probs, ub, qt, qts, dat, dats, normed, rscale, dn,
    t, r1, f, r2, zsend, rz,
    nall, call, n2, c2, a2, dq2, dkv2,
    p0, p1, rx0, rx1, fx0, fx1, sx0, sx1, y0, y1, ry0, ry1,
    pk, rk, ys0, ys1, ys2, z0, z1, z2, rz0, rz1, rz2,
    ssem, rsem, isem, osem,
):
    dp, seq = lax.axis_index("dp"), lax.axis_index("seq")
    x, zh, c = dp // 4, (dp // 2) % 2, dp % 2
    y, zl = seq // 4, seq % 4
    xs = (x, x + 1 - 2 * (x % 2), (x + 2) % 4, 3 - x)
    ys = (y, y + 1 - 2 * (y % 2), (y + 2) % 4, 3 - y)
    other = 1 - c

    def dev(x_=x, zh_=zh, c_=c, y_=y, zl_=zl):
        return (x_ * 4 + zh_ * 2 + c_, y_ * 4 + zl_)

    sent = []

    def send(name, src, dst, to):
        i = SLOT[name]
        copy = pltpu.make_async_remote_copy(
            src_ref=src, dst_ref=dst, send_sem=ssem.at[i], recv_sem=rsem.at[i],
            device_id=to, device_id_type=pl.DeviceIdType.MESH,
        )
        copy.start()
        sent.append(copy)
        return copy

    peers = [dev(c_=other)]
    peers += [dev(x_=xs[i], y_=ys[j]) for i in range(4) for j in range(4) if i or j]
    peers += [
        dev(zh_=(zh + a) % 2, zl_=(zl + b) % 4) for a in (0, 1) for b in range(4) if a or b
    ]
    loads = {}

    def load(i, name, src, dst):
        loads[name] = pltpu.make_async_copy(src, dst, isem.at[i])
        loads[name].start()

    load(0, "tok", tok_hbm, tok_ref)
    load(1, "gain", gain_hbm, gain_ref)
    load(2, "wkv", wkv_hbm, wkv_ref)
    barrier = pltpu.get_barrier_semaphore()
    for peer in peers:
        pl.semaphore_signal(barrier, inc=1, device_id=peer, device_id_type=pl.DeviceIdType.MESH)

    loads["tok"].wait()
    loads["gain"].wait()
    load(3, "wq", wq_hbm, wq_ref)
    load(4, "cot", cot_hbm, cot_ref)
    load(5, "wo", wo_hbm, wo_ref)
    load(6, "len", len_hbm, len_ref)
    gain = gain_ref[...].reshape(1, D)
    xf = tok_ref[...].astype(F32)
    rs = lax.rsqrt(jnp.mean(xf * xf, axis=-1, keepdims=True) + EPS)
    rscale[...] = rs
    nf = xf * rs * gain
    nb = nf.astype(BF16)
    normed[...] = nb
    loads["wkv"].wait()
    kvt[0, :, 0:ROWS] = mm(wkv_ref[...], nb, NT).astype(BF16)
    pl.semaphore_wait(barrier, len(peers))

    agz, agy, agr = {}, {}, {}
    lane = [slice(ROWS * d, ROWS * (d + 1)) for d in range(4)]

    def to_y(d):
        for j in (1, 3):
            agy[j, d] = send(("agy", j, d), kvt.at[0, :, lane[d]], kvt.at[j, :, lane[d]], dev(y_=ys[j]))

    def to_z(d):
        agz[d] = send(("agz", d), kvt.at[0, :, lane[0]], kvt.at[0, :, lane[d]], dev(zl_=(zl + 4 - d) % 4))

    def relay_y(d):
        j, to = ((1, 3), (1, 3), (3, 1), (3, 1))[d]
        agy[j, d].wait_recv()
        agr[d] = send(("agr", d), kvt.at[j, :, lane[d]], kvt.at[2, :, lane[d]], dev(y_=ys[to]))

    def wait_z(d):
        agz[d].wait_recv()
        to_y(d)

    to_z(1)
    to_z(3)
    to_y(0)
    to_z(2)
    loads["wq"].wait()
    q = mm(normed[...], wq_ref[...])
    for h in range(HEADS):
        qt[:, lane[h]] = q[:, lane[h]].T.astype(BF16)
    relay_y(0)
    loads["cot"].wait()
    loads["wo"].wait()
    for h in range(HEADS):
        da = mm(wo_ref[HV * h : HV * (h + 1), :], cot_ref[...], NT)
        dat[:, lane[h]] = da.astype(BF16)
    wait_z(1)
    wait_z(3)
    nall[...] = normed[...].T.reshape(4, 2, 2, 96, ROWS)
    wait_z(2)
    sib = dev(c_=other)
    sib_n = send(("sib", "n"), nall.at[:, :, other], n2.at[:, :, :, ROWS : 2 * ROWS], sib)
    n2[:, :, :, 0:ROWS] = nall[:, :, c]

    loads["len"].wait()
    length = len_ref[0]
    tops = [None]

    def score(j, d):
        first = (ys[j] * 4 + (zl + d) % 4) * ROWS
        blk = kvt[j, :, lane[d]]
        k = blk[0:HK, :].T
        vals[j, lane[d], :] = blk[HK:KV, :].T
        s = mm(k, qt[...]) * (SCALE * LOG2E)
        pos = first + lax.broadcasted_iota(jnp.int32, (ROWS, ALL), 0)
        s = jnp.where(pos < length, s, -1e30)
        scores[j, lane[d], :] = s
        part = jnp.max(s.reshape(ROWS // 8, 8, ALL), axis=0)
        tops[0] = part if tops[0] is None else jnp.maximum(tops[0], part)

    score(0, 0)
    score(0, 1)
    relay_y(1)
    score(0, 3)
    score(0, 2)
    relay_y(3)
    relay_y(2)
    for d, j in ((0, 1), (1, 1), (2, 3), (3, 3)):
        score(j, d)
    call[...] = cot_ref[...].T.reshape(4, 2, 2, 96, ROWS)
    sib_c = send(("sib", "c"), call.at[:, :, other], c2.at[:, :, :, ROWS : 2 * ROWS], sib)
    c2[:, :, :, 0:ROWS] = call[:, :, c]
    for j, d in ((3, 0), (3, 1), (1, 3), (1, 2)):
        agy[j, d].wait_recv()
        score(j, d)
    for d in (0, 1, 3, 2):
        agr[d].wait_recv()
        score(2, d)

    top = jnp.max(tops[0], axis=0, keepdims=True)
    total = jnp.zeros((8, ALL), F32)
    att = jnp.zeros((HV, ALL), F32)
    for j in range(4):
        for d in range(4):
            e = jnp.exp2(scores[j, lane[d], :] - top)
            total = total + jnp.sum(e.reshape(ROWS // 8, 8, ALL), axis=0)
            probs[j, lane[d], :] = e.astype(BF16)
        att = att + mm(kvt[j, HK:KV, :], probs[j])
    inv = 1.0 / jnp.sum(total, axis=0, keepdims=True)
    att_b = (att * inv).astype(BF16)
    da = dat[...].astype(F32)
    delta = jnp.sum(da * att_b.astype(F32), axis=0, keepdims=True)
    dats[...] = (da * inv).astype(BF16)
    qts[...] = (qt[...].astype(F32) * (inv * SCALE)).astype(BF16)
    for h in range(HEADS):
        a2[HV * h : HV * (h + 1), 0:ROWS] = att_b[:, lane[h]]
    mine, theirs = slice(0, ROWS), slice(ROWS, 2 * ROWS)
    sib_a = send(("sib", "a"), a2.at[:, mine], a2.at[:, theirs], sib)

    def backward(j, dq):
        for d in range(4):
            dpv = mm(vals[j, lane[d], :], dat[...])
            u = probs[j, lane[d], :].astype(F32) * (dpv - delta)
            ub[j, lane[d], :] = u.astype(BF16)
        dq = dq + mm(kvt[j, 0:HK, :], ub[j])
        t[j, 0:HK, :] = mm(qts[...], ub[j], NT).astype(BF16)
        t[j, HK:KV, :] = mm(dats[...], probs[j], NT).astype(BF16)
        return dq

    rs1, rs2, rsz = {}, {}, {}
    hop1, hop2 = (1, 1, 3, 3), (3, 3, 1, 1)

    def rs_opp(d):
        rs1[d, 1] = send(("rs1", d, 1), t.at[2, :, lane[d]], r1.at[d, 1], dev(y_=ys[hop1[d]]))

    def rs_own(d):
        rs1[d, 0] = send(("rs1", d, 0), t.at[hop1[d], :, lane[d]], r1.at[d, 0], dev(y_=ys[hop1[d]]))

    def rs_fwd(d):
        rs1[d, 1].wait_recv()
        f[d] = (t[hop2[d], :, lane[d]].astype(F32) + r1[d, 1].astype(F32)).astype(BF16)
        rs2[d] = send(("rs2", d), f.at[d], r2.at[d], dev(y_=ys[hop2[d]]))

    def rs_sum(d):
        rs1[d, 0].wait_recv()
        rs2[d].wait_recv()
        total = t[0, :, lane[d]].astype(F32) + r1[d, 0].astype(F32) + r2[d].astype(F32)
        zsend[d] = total.astype(BF16)
        if d:
            rsz[d] = send(("rsz", d), zsend.at[d], rz.at[d - 1], dev(zl_=(zl + d) % 4))

    part, rx, fx, sx = (p0, p1), (rx0, rx1), (fx0, fx1), (sx0, sx1)
    yb, ry, ysum = (y0, y1), (ry0, ry1), (ys0, ys1, ys2)
    zb, rzb = (z0, z1, z2), (rz0, rz1, rz2)
    grads, grads_hbm = (gwo_ref, gwq_ref, gwkv_ref), (gwo_hbm, gwq_hbm, gwkv_hbm)
    x1, x3 = dev(x_=xs[1]), dev(x_=xs[3])
    wx1, wx2, wy, wz = {}, {}, {}, {}

    def w_part(w, rows, right):
        for i in (2, 1, 3, 0):
            left = rows[xs[i]].reshape(192, 2 * ROWS)
            part[w][i] = mm(left, right[...], NT).reshape(2, 96, COLS[w]).astype(BF16)
            if i == 1:
                wx1[w, 0] = send(("wx1", w, 0), part[w].at[1:3, 0], rx[w].at[0], x1)
            if i == 3:
                wx1[w, 1] = send(("wx1", w, 1), part[w].at[2:4, 1], rx[w].at[1], x3)

    def w_x2(w):
        wx1[w, 0].wait_recv()
        fx[w][0] = (part[w][3, 0].astype(F32) + rx[w][0, 1].astype(F32)).astype(BF16)
        wx2[w, 0] = send(("wx2", w, 0), fx[w].at[0], sx[w].at[0], x3)
        wx1[w, 1].wait_recv()
        fx[w][1] = (part[w][1, 1].astype(F32) + rx[w][1, 0].astype(F32)).astype(BF16)
        wx2[w, 1] = send(("wx2", w, 1), fx[w].at[1], sx[w].at[1], x1)

    def w_y(w):
        sums = []
        for h in (0, 1):
            wx2[w, h].wait_recv()
            sums.append(
                part[w][0, h].astype(F32) + rx[w][h, h].astype(F32) + sx[w][h].astype(F32)
            )
        for k in range(4):
            rows = slice(24 * k, 24 * (k + 1))
            yb[w][k] = jnp.concatenate([sums[0][rows], sums[1][rows]], axis=0).astype(BF16)
        for j in (2, 1, 3):
            wy[w, j] = send(("wy", w, j), yb[w].at[ys[j]], ry[w].at[j - 1], dev(y_=ys[j]))

    wxy = {}

    def kv_part():
        for i in (2, 1, 3, 0):
            left = n2[xs[i]].reshape(192, 2 * ROWS)
            rows = mm(left, dkv2[...], NT)
            for k in range(4):
                piece = [rows[96 * h + 24 * k : 96 * h + 24 * (k + 1)] for h in (0, 1)]
                pk[i, k] = jnp.concatenate(piece, axis=0).astype(BF16)
            for j in (2, 1, 3, 0):
                if i or j:
                    wxy[i, j] = send(
                        ("wxy", i, j), pk.at[i, ys[j]], rk.at[4 * i + j], dev(x_=xs[i], y_=ys[j])
                    )

    def w_z(w):
        if w == 2:
            total = pk[0, y].astype(F32)
            for i in (0, 1, 3, 2):
                for j in (0, 1, 3, 2):
                    if i or j:
                        wxy[i, j].wait_recv()
                        total = total + rk[4 * i + j].astype(F32)
        else:
            total = yb[w][y].astype(F32)
            for j in (1, 3, 2):
                wy[w, j].wait_recv()
                total = total + ry[w][j - 1].astype(F32)
        ysum[w][...] = total
        zb[w][...] = jnp.zeros_like(zb[w])
        for k in range(8):
            zb[w][k, 0:6, :] = ysum[w][6 * k : 6 * (k + 1), :]
        for a, b in ((1, 0), (1, 1), (1, 3), (1, 2), (0, 2), (0, 1), (0, 3)):
            zh_, zl_ = (zh + a) % 2, (zl + b) % 4
            wz[w, a, b] = send(
                ("wz", w, a, b), zb[w].at[zh_ * 4 + zl_], rzb[w].at[a * 4 + b - 1], dev(zh_=zh_, zl_=zl_)
            )

    def w_end(w):
        total = zb[w][zh * 4 + zl]
        for a, b in ((0, 1), (0, 3), (0, 2), (1, 0), (1, 1), (1, 3), (1, 2)):
            wz[w, a, b].wait_recv()
            total = total + rzb[w][a * 4 + b - 1]
        grads[w][...] = total[0:6, :]

    dq = backward(2, jnp.zeros((HK, ALL), F32))
    for d in (1, 2, 0, 3):
        rs_opp(d)
    sib_c.wait_recv()
    sib_a.wait_recv()
    w_part(0, c2, a2)
    dq = backward(1, dq)
    rs_own(1)
    dq = backward(3, dq)
    rs_own(2)
    rs_fwd(1)
    rs_fwd(2)
    rs_own(0)
    rs_own(3)
    dq = backward(0, dq)
    dq_b = (dq * (inv * SCALE)).astype(BF16)
    for h in range(HEADS):
        dq2[HK * h : HK * (h + 1), mine] = dq_b[:, lane[h]]
    sib_q = send(("sib", "q"), dq2.at[:, mine], dq2.at[:, theirs], sib)
    rs_fwd(0)
    rs_fwd(3)
    sib_n.wait_recv()
    sib_q.wait_recv()
    w_part(1, n2, dq2)
    rs_sum(1)
    rs_sum(2)
    w_x2(0)
    rs_sum(3)
    rs_sum(0)
    w_x2(1)
    dqn = jnp.concatenate([dq2[HK * h : HK * (h + 1), mine].T for h in range(HEADS)], axis=1)
    dn[...] = mm(dqn, wq_ref[...], NT)
    w_y(0)
    dkv = zsend[0].astype(F32)
    for d in (1, 2, 3):
        rsz[d].wait_recv()
        dkv = dkv + rz[d - 1].astype(F32)
    dkv_b = dkv.astype(BF16)
    dkv2[:, mine] = dkv_b
    sib_kv = send(("sib", "kv"), dkv2.at[:, mine], dkv2.at[:, theirs], sib)
    dkvn = jnp.concatenate([dkv_b[0:HK].T, dkv_b[HK:KV].T], axis=1)
    dn[...] += mm(dkvn, wkv_ref[...])
    sib_kv.wait_recv()
    kv_part()
    w_y(1)
    xf = tok_ref[...].astype(F32)
    rs = rscale[...]
    gd = gain_ref[...].reshape(1, D) * dn[...]
    inner = jnp.mean(xf * gd, axis=-1, keepdims=True)
    out = cot_ref[...].astype(F32) + rs * gd - xf * (rs * rs * rs * inner)
    gtok_ref[...] = out.astype(BF16)
    stores = [pltpu.make_async_copy(gtok_ref, gtok_hbm, osem.at[3])]
    stores[0].start()
    w_z(0)
    w_z(1)
    w_z(2)
    for w in range(3):
        w_end(w)
        stores.append(pltpu.make_async_copy(grads[w], grads_hbm[w], osem.at[w]))
        stores[-1].start()
    for copy in sent:
        copy.wait_send()
    for copy in stores:
        copy.wait()


def hand_on(*refs):
    come, go = refs[12], refs[13]
    first = [pltpu.make_async_copy(refs[i], refs[8 + i], come.at[i]) for i in range(4)]
    second = [pltpu.make_async_copy(refs[8 + i], refs[4 + i], go.at[i]) for i in range(4)]
    for copy in first:
        copy.start()
    for i in range(4):
        first[i].wait()
        second[i].start()
    for copy in second:
        copy.wait()


def body(tokens, lengths, cotangent, gain, w_q, w_kv, w_o):
    hbm = pl.BlockSpec(memory_space=pltpu.HBM)

    def per_weight(shape, kind):
        return [pltpu.VMEM(shape(n), kind) for n in COLS]

    scratch = [
        pltpu.SMEM((1,), jnp.int32),
        pltpu.VMEM((ROWS, D), BF16),
        pltpu.VMEM((ROWS, D), BF16),
        pltpu.VMEM((D,), F32),
        pltpu.VMEM((D, COLS[1]), BF16),
        pltpu.VMEM((KV, D), BF16),
        pltpu.VMEM((HEADS * HV, D), BF16),
        pltpu.VMEM((ROWS, D), BF16),
        pltpu.VMEM((6, COLS[1]), F32),
        pltpu.VMEM((6, COLS[2]), F32),
        pltpu.VMEM((6, COLS[0]), F32),
        pltpu.VMEM((4, KV, CHUNK), BF16),
        pltpu.VMEM((4, CHUNK, HV), BF16),
        pltpu.VMEM((4, CHUNK, ALL), F32),
        pltpu.VMEM((4, CHUNK, ALL), BF16),
        pltpu.VMEM((4, CHUNK, ALL), BF16),
        pltpu.VMEM((HK, ALL), BF16),
        pltpu.VMEM((HK, ALL), BF16),
        pltpu.VMEM((HV, ALL), BF16),
        pltpu.VMEM((HV, ALL), BF16),
        pltpu.VMEM((ROWS, D), BF16),
        pltpu.VMEM((ROWS, 1), F32),
        pltpu.VMEM((ROWS, D), F32),
        pltpu.VMEM((4, KV, CHUNK), BF16),
        pltpu.VMEM((4, 2, KV, ROWS), BF16),
        pltpu.VMEM((4, KV, ROWS), BF16),
        pltpu.VMEM((4, KV, ROWS), BF16),
        pltpu.VMEM((4, KV, ROWS), BF16),
        pltpu.VMEM((3, KV, ROWS), BF16),
        pltpu.VMEM((4, 2, 2, 96, ROWS), BF16),
        pltpu.VMEM((4, 2, 2, 96, ROWS), BF16),
        pltpu.VMEM((4, 2, 96, 2 * ROWS), BF16),
        pltpu.VMEM((4, 2, 96, 2 * ROWS), BF16),
        pltpu.VMEM((COLS[0], 2 * ROWS), BF16),
        pltpu.VMEM((COLS[1], 2 * ROWS), BF16),
        pltpu.VMEM((COLS[2], 2 * ROWS), BF16),
    ]
    scratch += per_weight(lambda n: (4, 2, 96, n), BF16)[:2]
    scratch += per_weight(lambda n: (2, 2, 96, n), BF16)[:2]
    scratch += per_weight(lambda n: (2, 96, n), BF16)[:2]
    scratch += per_weight(lambda n: (2, 96, n), BF16)[:2]
    scratch += per_weight(lambda n: (4, 48, n), BF16)[:2]
    scratch += per_weight(lambda n: (3, 48, n), BF16)[:2]
    scratch += [pltpu.VMEM((4, 4, 48, KV), BF16), pltpu.VMEM((16, 48, KV), BF16)]
    scratch += per_weight(lambda n: (48, n), F32)
    scratch += per_weight(lambda n: (8, 8, n), F32)
    scratch += per_weight(lambda n: (7, 8, n), F32)
    scratch += [pltpu.SemaphoreType.DMA((len(SLOT),)), pltpu.SemaphoreType.DMA((len(SLOT),))]
    scratch += [pltpu.SemaphoreType.DMA((7,)), pltpu.SemaphoreType.DMA((4,))]
    results = (
        jax.ShapeDtypeStruct((ROWS, D), BF16),
        jax.ShapeDtypeStruct((6, COLS[1]), F32),
        jax.ShapeDtypeStruct((6, COLS[2]), F32),
        jax.ShapeDtypeStruct((6, COLS[0]), F32),
    )
    outs = pl.pallas_call(
        kernel,
        out_shape=results,
        in_specs=[hbm] * 7,
        out_specs=(hbm,) * 4,
        scratch_shapes=scratch,
        compiler_params=pltpu.CompilerParams(
            collective_id=0, has_side_effects=True, vmem_limit_bytes=56 * 1024 * 1024
        ),
    )(lengths, tokens[0], cotangent[0], gain, w_q, w_kv.T, w_o)
    grad_x, grad_wq, grad_wkv, grad_wo_t = pl.pallas_call(
        hand_on,
        out_shape=results,
        in_specs=[hbm] * 4,
        out_specs=(hbm,) * 4,
        scratch_shapes=[pltpu.VMEM(r.shape, r.dtype) for r in results]
        + [pltpu.SemaphoreType.DMA((4,)), pltpu.SemaphoreType.DMA((4,))],
        compiler_params=pltpu.CompilerParams(vmem_limit_bytes=60 * 1024 * 1024),
    )(*outs)
    return grad_x[None], grad_wq, grad_wkv, grad_wo_t


def solution(mesh):
    return jax.shard_map(
        body,
        mesh=mesh,
        in_specs=(P("dp", "seq", None), P("dp"), P("dp", "seq", None), P(), P(), P(), P()),
        out_specs=(
            P("dp", "seq", None),
            P(("dp", "seq"), None),
            P(("dp", "seq"), None),
            P(("dp", "seq"), None),
        ),
        check_vma=False,
    )
```

```python
import functools

import jax
import jax.numpy as jnp
from jax import lax
from jax.experimental import pallas as pl
from jax.experimental.pallas import tpu as pltpu
from jax.sharding import PartitionSpec as P

EPS = 1e-06
HK = 128
HV = 192
HEADS = 4
KV = HK + HV
D = 1536
ROWS = 128
ALL = HEADS * ROWS
CHUNK = 512
LOG2E = 1.4426950408889634
SCALE = HK ** (-0.5)
F32 = jnp.float32
BF16 = jnp.bfloat16
NT = (((1,), (1,)), ((), ()))
NN = (((1,), (0,)), ((), ()))

COLS = (HEADS * HV, HEADS * HK, KV)
HALF = (384, 256, 256)


def mm(a, b, dims=NN):
    return lax.dot_general(a, b, dims, preferred_element_type=F32)


def make_slots():
    names = []
    names += [("agz", d) for d in (1, 2, 3)]
    names += [("agy", j, d) for j in (1, 3) for d in range(4)]
    names += [("agr", d) for d in range(4)]
    names += [("sib", k) for k in ("n", "c", "a", "q", "kv")]
    names += [("rs1", d, k) for d in range(4) for k in (0, 1)]
    names += [("rs2", d) for d in range(4)]
    names += [("rsz", d) for d in (1, 2, 3)]
    for w in range(2):
        names += [(k, w, h) for k in ("xd", "xf") for h in (0, 1)]
        names += [("xn", w, h, b) for h in (0, 1) for b in (0, 1)]
        names += [("wx2", w, h) for h in (0, 1)]
        names += [("wy", w, j) for j in (1, 2, 3)]
    names += [("wxy", i, j) for i in range(4) for j in range(4) if i or j]
    for w in range(3):
        names += [("wz", w, a, b) for a in (0, 1) for b in range(4) if a or b]
    return {name: i for i, name in enumerate(names)}


SLOT = make_slots()


def kernel(
    len_hbm, tok_hbm, cot_hbm, gain_hbm, wq_hbm, wkv_hbm, wo_hbm,
    gtok_hbm, gwq_hbm, gwkv_hbm, gwo_hbm,
    len_ref, tok_ref, cot_ref, gain_ref, wq_ref, wkv_ref, wo_ref,
    gtok_ref, gwq_ref, gwkv_ref, gwo_ref,
    kvt, vals, scores, probs, ub, qt, qts, dat, dats, normed, rscale, dn,
    t, r1, f, r2, zsend, rz,
    nall, call, n2, c2, a2, dq2, dkv2,
    n4, c4, a4, dq4, po0, po1, pf0, pf1, sx0, sx1, y0, y1, ry0, ry1,
    pk, rk, ys0, ys1, ys2, z0, z1, z2, rz0, rz1, rz2,
    ssem, rsem, isem, osem,
):
    dp, seq = lax.axis_index("dp"), lax.axis_index("seq")
    x, zh, c = dp // 4, (dp // 2) % 2, dp % 2
    y, zl = seq // 4, seq % 4
    xs = (x, x + 1 - 2 * (x % 2), (x + 2) % 4, 3 - x)
    ys = (y, y + 1 - 2 * (y % 2), (y + 2) % 4, 3 - y)
    other = 1 - c

    def dev(x_=x, zh_=zh, c_=c, y_=y, zl_=zl):
        return (x_ * 4 + zh_ * 2 + c_, y_ * 4 + zl_)

    sent = []

    def send(name, src, dst, to):
        i = SLOT[name]
        copy = pltpu.make_async_remote_copy(
            src_ref=src, dst_ref=dst, send_sem=ssem.at[i], recv_sem=rsem.at[i],
            device_id=to, device_id_type=pl.DeviceIdType.MESH,
        )
        copy.start()
        sent.append(copy)
        return copy

    peers = [dev(c_=other)]
    peers += [dev(x_=xs[i], y_=ys[j]) for i in range(4) for j in range(4) if i or j]
    peers += [
        dev(zh_=(zh + a) % 2, zl_=(zl + b) % 4) for a in (0, 1) for b in range(4) if a or b
    ]
    loads = {}

    def load(i, name, src, dst):
        loads[name] = pltpu.make_async_copy(src, dst, isem.at[i])
        loads[name].start()

    load(0, "tok", tok_hbm, tok_ref)
    load(1, "gain", gain_hbm, gain_ref)
    load(2, "wkv", wkv_hbm, wkv_ref)
    barrier = pltpu.get_barrier_semaphore()
    for peer in peers:
        pl.semaphore_signal(barrier, inc=1, device_id=peer, device_id_type=pl.DeviceIdType.MESH)

    loads["tok"].wait()
    loads["gain"].wait()
    load(3, "wq", wq_hbm, wq_ref)
    load(4, "cot", cot_hbm, cot_ref)
    load(5, "wo", wo_hbm, wo_ref)
    load(6, "len", len_hbm, len_ref)
    gain = gain_ref[...].reshape(1, D)
    xf = tok_ref[...].astype(F32)
    rs = lax.rsqrt(jnp.mean(xf * xf, axis=-1, keepdims=True) + EPS)
    rscale[...] = rs
    nf = xf * rs * gain
    nb = nf.astype(BF16)
    normed[...] = nb
    loads["wkv"].wait()
    kvt[0, :, 0:ROWS] = mm(wkv_ref[...], nb, NT).astype(BF16)
    pl.semaphore_wait(barrier, len(peers))

    agz, agy, agr = {}, {}, {}
    lane = [slice(ROWS * d, ROWS * (d + 1)) for d in range(4)]

    def to_y(d):
        for j in (1, 3):
            agy[j, d] = send(("agy", j, d), kvt.at[0, :, lane[d]], kvt.at[j, :, lane[d]], dev(y_=ys[j]))

    def to_z(d):
        agz[d] = send(("agz", d), kvt.at[0, :, lane[0]], kvt.at[0, :, lane[d]], dev(zl_=(zl + 4 - d) % 4))

    def relay_y(d):
        j, to = ((1, 3), (1, 3), (3, 1), (3, 1))[d]
        agy[j, d].wait_recv()
        agr[d] = send(("agr", d), kvt.at[j, :, lane[d]], kvt.at[2, :, lane[d]], dev(y_=ys[to]))

    def wait_z(d):
        agz[d].wait_recv()
        to_y(d)

    to_z(1)
    to_z(3)
    to_y(0)
    to_z(2)
    loads["wq"].wait()
    q = mm(normed[...], wq_ref[...])
    for h in range(HEADS):
        qt[:, lane[h]] = q[:, lane[h]].T.astype(BF16)
    relay_y(0)
    loads["cot"].wait()
    loads["wo"].wait()
    for h in range(HEADS):
        da = mm(wo_ref[HV * h : HV * (h + 1), :], cot_ref[...], NT)
        dat[:, lane[h]] = da.astype(BF16)
    sib = dev(c_=other)
    nall[...] = normed[...].T.reshape(4, 2, 2, 96, ROWS)
    sib_n = send(("sib", "n"), nall.at[:, :, other], n2.at[:, :, :, ROWS : 2 * ROWS], sib)
    n2[:, :, :, 0:ROWS] = nall[:, :, c]
    call[...] = cot_ref[...].T.reshape(4, 2, 2, 96, ROWS)
    sib_c = send(("sib", "c"), call.at[:, :, other], c2.at[:, :, :, ROWS : 2 * ROWS], sib)
    c2[:, :, :, 0:ROWS] = call[:, :, c]
    wait_z(1)
    wait_z(3)

    x1, x3 = dev(x_=xs[1]), dev(x_=xs[3])
    xd, xf, xn = {}, {}, {}

    def to_x(w, rows, rows4):
        for h, near, to in ((0, 1, x1), (1, 3, x3)):
            for b, i in ((0, near), (1, 2)):
                xn[w, h, b] = send(("xn", w, h, b), rows.at[xs[i], h], rows4.at[h, b], to)

    sib_n.wait_recv()
    to_x(1, n2, n4)
    sib_c.wait_recv()
    to_x(0, c2, c4)
    wait_z(2)

    loads["len"].wait()
    length = len_ref[0]
    tops = [None]

    def score(j, d):
        first = (ys[j] * 4 + (zl + d) % 4) * ROWS
        blk = kvt[j, :, lane[d]]
        k = blk[0:HK, :].T
        vals[j, lane[d], :] = blk[HK:KV, :].T
        s = mm(k, qt[...]) * (SCALE * LOG2E)
        pos = first + lax.broadcasted_iota(jnp.int32, (ROWS, ALL), 0)
        s = jnp.where(pos < length, s, -1e30)
        scores[j, lane[d], :] = s
        part = jnp.max(s.reshape(ROWS // 8, 8, ALL), axis=0)
        tops[0] = part if tops[0] is None else jnp.maximum(tops[0], part)

    score(0, 0)
    score(0, 1)
    relay_y(1)
    score(0, 3)
    score(0, 2)
    relay_y(3)
    relay_y(2)
    for d, j in ((0, 1), (1, 1), (2, 3), (3, 3)):
        score(j, d)
    for j, d in ((3, 0), (3, 1), (1, 3), (1, 2)):
        agy[j, d].wait_recv()
        score(j, d)
    for d in (0, 1, 3, 2):
        agr[d].wait_recv()
        score(2, d)

    top = jnp.max(tops[0], axis=0, keepdims=True)
    total = jnp.zeros((8, ALL), F32)
    att = jnp.zeros((HV, ALL), F32)
    for j in range(4):
        for d in range(4):
            e = jnp.exp2(scores[j, lane[d], :] - top)
            total = total + jnp.sum(e.reshape(ROWS // 8, 8, ALL), axis=0)
            probs[j, lane[d], :] = e.astype(BF16)
        att = att + mm(kvt[j, HK:KV, :], probs[j])
    inv = 1.0 / jnp.sum(total, axis=0, keepdims=True)
    att_b = (att * inv).astype(BF16)
    da = dat[...].astype(F32)
    delta = jnp.sum(da * att_b.astype(F32), axis=0, keepdims=True)
    dats[...] = (da * inv).astype(BF16)
    qts[...] = (qt[...].astype(F32) * (inv * SCALE)).astype(BF16)
    for h in range(HEADS):
        a2[HV * h : HV * (h + 1), 0:ROWS] = att_b[:, lane[h]]
    mine, theirs = slice(0, ROWS), slice(ROWS, 2 * ROWS)
    def share(w, right, right4):
        for h, to in ((0, x1), (1, x3)):
            xd[w, h] = send(("xd", w, h), right.at[:, mine], right4.at[h, :, mine], to)

    def share_on(w, right4):
        for h in (0, 1):
            xd[w, h].wait_recv()
            xf[w, h] = send(("xf", w, h), right4.at[h, :, mine], right4.at[h, :, theirs], sib)

    sib_a = send(("sib", "a"), a2.at[:, mine], a2.at[:, theirs], sib)
    share(0, a2, a4)

    def backward(j, dq):
        for d in range(4):
            dpv = mm(vals[j, lane[d], :], dat[...])
            u = probs[j, lane[d], :].astype(F32) * (dpv - delta)
            ub[j, lane[d], :] = u.astype(BF16)
        dq = dq + mm(kvt[j, 0:HK, :], ub[j])
        t[j, 0:HK, :] = mm(qts[...], ub[j], NT).astype(BF16)
        t[j, HK:KV, :] = mm(dats[...], probs[j], NT).astype(BF16)
        return dq

    rs1, rs2, rsz = {}, {}, {}
    hop1, hop2 = (1, 1, 3, 3), (3, 3, 1, 1)

    def rs_opp(d):
        rs1[d, 1] = send(("rs1", d, 1), t.at[2, :, lane[d]], r1.at[d, 1], dev(y_=ys[hop1[d]]))

    def rs_own(d):
        rs1[d, 0] = send(("rs1", d, 0), t.at[hop1[d], :, lane[d]], r1.at[d, 0], dev(y_=ys[hop1[d]]))

    def rs_fwd(d):
        rs1[d, 1].wait_recv()
        f[d] = (t[hop2[d], :, lane[d]].astype(F32) + r1[d, 1].astype(F32)).astype(BF16)
        rs2[d] = send(("rs2", d), f.at[d], r2.at[d], dev(y_=ys[hop2[d]]))

    def rs_sum(d):
        rs1[d, 0].wait_recv()
        rs2[d].wait_recv()
        total = t[0, :, lane[d]].astype(F32) + r1[d, 0].astype(F32) + r2[d].astype(F32)
        zsend[d] = total.astype(BF16)
        if d:
            rsz[d] = send(("rsz", d), zsend.at[d], rz.at[d - 1], dev(zl_=(zl + d) % 4))

    po, pf, sx = (po0, po1), (pf0, pf1), (sx0, sx1)
    yb, ry, ysum = (y0, y1), (ry0, ry1), (ys0, ys1, ys2)
    zb, rzb = (z0, z1, z2), (rz0, rz1, rz2)
    grads, grads_hbm = (gwo_ref, gwq_ref, gwkv_ref), (gwo_hbm, gwq_hbm, gwkv_hbm)
    wx2, wy, wz = {}, {}, {}

    def w_part(w, rows, rows4, right, right4):
        for h, far, to in ((0, 3, x3), (1, 1, x1)):
            left = jnp.concatenate([rows[xs[far], h], rows[x, h]], axis=0)
            xn[w, h, 0].wait_recv()
            xn[w, h, 1].wait_recv()
            left4 = jnp.concatenate([rows4[h, 1], rows4[h, 0]], axis=0)
            xf[w, h].wait_recv()
            both = mm(left, right[...], NT) + mm(left4, right4[h], NT)
            pf[w][h] = both[0:96].astype(BF16)
            wx2[w, h] = send(("wx2", w, h), pf[w].at[h], sx[w].at[h], to)
            po[w][h] = both[96:192]

    def w_y(w):
        sums = []
        for h in (0, 1):
            wx2[w, h].wait_recv()
            sums.append(po[w][h] + sx[w][h].astype(F32))
        for k in range(4):
            rows = slice(24 * k, 24 * (k + 1))
            yb[w][k] = jnp.concatenate([sums[0][rows], sums[1][rows]], axis=0).astype(BF16)
        for j in (2, 1, 3):
            wy[w, j] = send(("wy", w, j), yb[w].at[ys[j]], ry[w].at[j - 1], dev(y_=ys[j]))

    wxy = {}

    def kv_part():
        for i in (2, 1, 3, 0):
            left = n2[xs[i]].reshape(192, 2 * ROWS)
            rows = mm(left, dkv2[...], NT)
            for k in range(4):
                piece = [rows[96 * h + 24 * k : 96 * h + 24 * (k + 1)] for h in (0, 1)]
                pk[i, k] = jnp.concatenate(piece, axis=0).astype(BF16)
            for j in (2, 1, 3, 0):
                if i or j:
                    wxy[i, j] = send(
                        ("wxy", i, j), pk.at[i, ys[j]], rk.at[4 * i + j], dev(x_=xs[i], y_=ys[j])
                    )

    def w_z(w):
        if w == 2:
            total = pk[0, y].astype(F32)
            for i in (0, 1, 3, 2):
                for j in (0, 1, 3, 2):
                    if i or j:
                        wxy[i, j].wait_recv()
                        total = total + rk[4 * i + j].astype(F32)
        else:
            total = yb[w][y].astype(F32)
            for j in (1, 3, 2):
                wy[w, j].wait_recv()
                total = total + ry[w][j - 1].astype(F32)
        ysum[w][0:48, :] = total
        ysum[w][48:56, :] = jnp.zeros((8, COLS[w]), F32)
        for k in range(8):
            rows = ysum[w][6 * k : 6 * k + 8, :]
            right = rows[:, HALF[w] :]
            if right.shape[1] < HALF[w]:
                right = jnp.concatenate([right, jnp.zeros((8, HALF[w] - right.shape[1]), F32)], axis=1)
            zb[w][k] = jnp.concatenate([rows[:, : HALF[w]], right], axis=0).astype(BF16)
        for a, b in ((1, 0), (1, 1), (1, 3), (1, 2), (0, 2), (0, 1), (0, 3)):
            zh_, zl_ = (zh + a) % 2, (zl + b) % 4
            wz[w, a, b] = send(
                ("wz", w, a, b), zb[w].at[zh_ * 4 + zl_], rzb[w].at[a * 4 + b - 1], dev(zh_=zh_, zl_=zl_)
            )

    def w_end(w):
        total = zb[w][zh * 4 + zl].astype(F32)
        for a, b in ((0, 1), (0, 3), (0, 2), (1, 0), (1, 1), (1, 3), (1, 2)):
            wz[w, a, b].wait_recv()
            total = total + rzb[w][a * 4 + b - 1].astype(F32)
        grads[w][:, : HALF[w]] = total[0:6]
        grads[w][:, HALF[w] :] = total[8:14, : COLS[w] - HALF[w]]

    dq = backward(2, jnp.zeros((HK, ALL), F32))
    for d in (1, 2, 0, 3):
        rs_opp(d)
    dq = backward(1, dq)
    rs_own(1)
    dq = backward(3, dq)
    rs_own(2)
    dq = backward(0, dq)
    dq_b = (dq * (inv * SCALE)).astype(BF16)
    for h in range(HEADS):
        dq2[HK * h : HK * (h + 1), mine] = dq_b[:, lane[h]]
    sib_q = send(("sib", "q"), dq2.at[:, mine], dq2.at[:, theirs], sib)
    share(1, dq2, dq4)
    rs_fwd(1)
    rs_fwd(2)
    rs_own(0)
    rs_own(3)
    share_on(0, a4)
    rs_fwd(0)
    rs_fwd(3)
    sib_a.wait_recv()
    w_part(0, c2, c4, a2, a4)
    rs_sum(1)
    rs_sum(2)
    share_on(1, dq4)
    sib_q.wait_recv()
    w_part(1, n2, n4, dq2, dq4)
    rs_sum(3)
    rs_sum(0)
    dqn = jnp.concatenate([dq2[HK * h : HK * (h + 1), mine].T for h in range(HEADS)], axis=1)
    dn[...] = mm(dqn, wq_ref[...], NT)
    w_y(0)
    dkv = zsend[0].astype(F32)
    for d in (1, 2, 3):
        rsz[d].wait_recv()
        dkv = dkv + rz[d - 1].astype(F32)
    dkv_b = dkv.astype(BF16)
    dkv2[:, mine] = dkv_b
    sib_kv = send(("sib", "kv"), dkv2.at[:, mine], dkv2.at[:, theirs], sib)
    dkvn = jnp.concatenate([dkv_b[0:HK].T, dkv_b[HK:KV].T], axis=1)
    dn[...] += mm(dkvn, wkv_ref[...])
    w_y(1)
    sib_kv.wait_recv()
    kv_part()
    xf = tok_ref[...].astype(F32)
    rs = rscale[...]
    gd = gain_ref[...].reshape(1, D) * dn[...]
    inner = jnp.mean(xf * gd, axis=-1, keepdims=True)
    out = cot_ref[...].astype(F32) + rs * gd - xf * (rs * rs * rs * inner)
    gtok_ref[...] = out.astype(BF16)
    stores = [pltpu.make_async_copy(gtok_ref, gtok_hbm, osem.at[3])]
    stores[0].start()
    w_z(0)
    w_z(1)
    w_z(2)
    for w in range(3):
        w_end(w)
        stores.append(pltpu.make_async_copy(grads[w], grads_hbm[w], osem.at[w]))
        stores[-1].start()
    for copy in sent:
        copy.wait_send()
    for copy in stores:
        copy.wait()


def hand_on(*refs):
    come, go = refs[12], refs[13]
    first = [pltpu.make_async_copy(refs[i], refs[8 + i], come.at[i]) for i in range(4)]
    second = [pltpu.make_async_copy(refs[8 + i], refs[4 + i], go.at[i]) for i in range(4)]
    for copy in first:
        copy.start()
    for i in range(4):
        first[i].wait()
        second[i].start()
    for copy in second:
        copy.wait()


def body(tokens, lengths, cotangent, gain, w_q, w_kv, w_o):
    hbm = pl.BlockSpec(memory_space=pltpu.HBM)

    def per_weight(shape, kind):
        return [pltpu.VMEM(shape(n), kind) for n in COLS]

    scratch = [
        pltpu.SMEM((1,), jnp.int32),
        pltpu.VMEM((ROWS, D), BF16),
        pltpu.VMEM((ROWS, D), BF16),
        pltpu.VMEM((D,), F32),
        pltpu.VMEM((D, COLS[1]), BF16),
        pltpu.VMEM((KV, D), BF16),
        pltpu.VMEM((HEADS * HV, D), BF16),
        pltpu.VMEM((ROWS, D), BF16),
        pltpu.VMEM((6, COLS[1]), F32),
        pltpu.VMEM((6, COLS[2]), F32),
        pltpu.VMEM((6, COLS[0]), F32),
        pltpu.VMEM((4, KV, CHUNK), BF16),
        pltpu.VMEM((4, CHUNK, HV), BF16),
        pltpu.VMEM((4, CHUNK, ALL), F32),
        pltpu.VMEM((4, CHUNK, ALL), BF16),
        pltpu.VMEM((4, CHUNK, ALL), BF16),
        pltpu.VMEM((HK, ALL), BF16),
        pltpu.VMEM((HK, ALL), BF16),
        pltpu.VMEM((HV, ALL), BF16),
        pltpu.VMEM((HV, ALL), BF16),
        pltpu.VMEM((ROWS, D), BF16),
        pltpu.VMEM((ROWS, 1), F32),
        pltpu.VMEM((ROWS, D), F32),
        pltpu.VMEM((4, KV, CHUNK), BF16),
        pltpu.VMEM((4, 2, KV, ROWS), BF16),
        pltpu.VMEM((4, KV, ROWS), BF16),
        pltpu.VMEM((4, KV, ROWS), BF16),
        pltpu.VMEM((4, KV, ROWS), BF16),
        pltpu.VMEM((3, KV, ROWS), BF16),
        pltpu.VMEM((4, 2, 2, 96, ROWS), BF16),
        pltpu.VMEM((4, 2, 2, 96, ROWS), BF16),
        pltpu.VMEM((4, 2, 96, 2 * ROWS), BF16),
        pltpu.VMEM((4, 2, 96, 2 * ROWS), BF16),
        pltpu.VMEM((COLS[0], 2 * ROWS), BF16),
        pltpu.VMEM((COLS[1], 2 * ROWS), BF16),
        pltpu.VMEM((COLS[2], 2 * ROWS), BF16),
    ]
    scratch += [pltpu.VMEM((2, 2, 96, 2 * ROWS), BF16)] * 2
    scratch += per_weight(lambda n: (2, n, 2 * ROWS), BF16)[:2]
    scratch += per_weight(lambda n: (2, 96, n), F32)[:2]
    scratch += per_weight(lambda n: (2, 96, n), BF16)[:2]
    scratch += per_weight(lambda n: (2, 96, n), BF16)[:2]
    scratch += per_weight(lambda n: (4, 48, n), BF16)[:2]
    scratch += per_weight(lambda n: (3, 48, n), BF16)[:2]
    scratch += [pltpu.VMEM((4, 4, 48, KV), BF16), pltpu.VMEM((16, 48, KV), BF16)]
    scratch += per_weight(lambda n: (56, n), F32)
    scratch += [pltpu.VMEM((8, 16, n), BF16) for n in HALF]
    scratch += [pltpu.VMEM((7, 16, n), BF16) for n in HALF]
    scratch += [pltpu.SemaphoreType.DMA((len(SLOT),)), pltpu.SemaphoreType.DMA((len(SLOT),))]
    scratch += [pltpu.SemaphoreType.DMA((7,)), pltpu.SemaphoreType.DMA((4,))]
    results = (
        jax.ShapeDtypeStruct((ROWS, D), BF16),
        jax.ShapeDtypeStruct((6, COLS[1]), F32),
        jax.ShapeDtypeStruct((6, COLS[2]), F32),
        jax.ShapeDtypeStruct((6, COLS[0]), F32),
    )
    outs = pl.pallas_call(
        kernel,
        out_shape=results,
        in_specs=[hbm] * 7,
        out_specs=(hbm,) * 4,
        scratch_shapes=scratch,
        compiler_params=pltpu.CompilerParams(
            collective_id=0, has_side_effects=True, vmem_limit_bytes=56 * 1024 * 1024
        ),
    )(lengths, tokens[0], cotangent[0], gain, w_q, w_kv.T, w_o)
    grad_x, grad_wq, grad_wkv, grad_wo_t = pl.pallas_call(
        hand_on,
        out_shape=results,
        in_specs=[hbm] * 4,
        out_specs=(hbm,) * 4,
        scratch_shapes=[pltpu.VMEM(r.shape, r.dtype) for r in results]
        + [pltpu.SemaphoreType.DMA((4,)), pltpu.SemaphoreType.DMA((4,))],
        compiler_params=pltpu.CompilerParams(vmem_limit_bytes=60 * 1024 * 1024),
    )(*outs)
    return grad_x[None], grad_wq, grad_wkv, grad_wo_t


def solution(mesh):
    return jax.shard_map(
        body,
        mesh=mesh,
        in_specs=(P("dp", "seq", None), P("dp"), P("dp", "seq", None), P(), P(), P(), P()),
        out_specs=(
            P("dp", "seq", None),
            P(("dp", "seq"), None),
            P(("dp", "seq"), None),
            P(("dp", "seq"), None),
        ),
        check_vma=False,
    )
```

```python
import functools

import jax
import jax.numpy as jnp
from jax import lax
from jax.experimental import pallas as pl
from jax.experimental.pallas import tpu as pltpu
from jax.sharding import PartitionSpec as P

EPS = 1e-06
HK = 128
HV = 192
HEADS = 4
KV = HK + HV
D = 1536
ROWS = 128
ALL = HEADS * ROWS
CHUNK = 512
LOG2E = 1.4426950408889634
SCALE = HK ** (-0.5)
F32 = jnp.float32
BF16 = jnp.bfloat16
NT = (((1,), (1,)), ((), ()))
NN = (((1,), (0,)), ((), ()))

COLS = (HEADS * HV, HEADS * HK, KV)
HALF = (384, 256, 256)


def mm(a, b, dims=NN):
    return lax.dot_general(a, b, dims, preferred_element_type=F32)


def make_slots():
    names = []
    names += [("agz", d, p) for d in (1, 2, 3) for p in (0, 1)]
    names += [("agy", j, d, p) for j in (1, 3) for d in range(4) for p in (0, 1)]
    names += [("agr", d, p) for d in range(4) for p in (0, 1)]
    names += [("sib", k) for k in ("n", "c", "a", "q", "kv")]
    names += [("rs1", d, k) for d in range(4) for k in (0, 1)]
    names += [("rs2", d) for d in range(4)]
    names += [("rsz", d) for d in (1, 2, 3)]
    for w in range(2):
        names += [(k, w, h) for k in ("xd", "xf") for h in (0, 1)]
        names += [("xn", w, h, b) for h in (0, 1) for b in (0, 1)]
        names += [("wx2", w, h) for h in (0, 1)]
        names += [("wy", w, j) for j in (1, 2, 3)]
    names += [("wxy", i, j) for i in range(4) for j in range(4) if i or j]
    for w in range(3):
        names += [("wz", w, a, b) for a in (0, 1) for b in range(4) if a or b]
    return {name: i for i, name in enumerate(names)}


SLOT = make_slots()


def kernel(
    len_hbm, tok_hbm, cot_hbm, gain_hbm, wq_hbm, wkv_hbm, wo_hbm,
    gtok_hbm, gwq_hbm, gwkv_hbm, gwo_hbm,
    len_ref, tok_ref, cot_ref, gain_ref, wq_ref, wkv_ref, wo_ref,
    gtok_ref, gwq_ref, gwkv_ref, gwo_ref,
    kvt, vals, scores, probs, ub, qt, qts, dat, dats, normed, rscale, dn,
    t, r1, f, r2, zsend, rz,
    nall, call, n2, c2, a2, dq2, dkv2,
    n4, c4, a4, dq4, po0, po1, pf0, pf1, sx0, sx1, y0, y1, ry0, ry1,
    pk, rk, ys0, ys1, ys2, z0, z1, z2, rz0, rz1, rz2,
    ssem, rsem, isem, osem,
):
    dp, seq = lax.axis_index("dp"), lax.axis_index("seq")
    x, zh, c = dp // 4, (dp // 2) % 2, dp % 2
    y, zl = seq // 4, seq % 4
    xs = (x, x + 1 - 2 * (x % 2), (x + 2) % 4, 3 - x)
    ys = (y, y + 1 - 2 * (y % 2), (y + 2) % 4, 3 - y)
    other = 1 - c

    def dev(x_=x, zh_=zh, c_=c, y_=y, zl_=zl):
        return (x_ * 4 + zh_ * 2 + c_, y_ * 4 + zl_)

    sent = []

    def send(name, src, dst, to):
        i = SLOT[name]
        copy = pltpu.make_async_remote_copy(
            src_ref=src, dst_ref=dst, send_sem=ssem.at[i], recv_sem=rsem.at[i],
            device_id=to, device_id_type=pl.DeviceIdType.MESH,
        )
        copy.start()
        sent.append(copy)
        return copy

    peers = [dev(c_=other)]
    peers += [dev(x_=xs[i], y_=ys[j]) for i in range(4) for j in range(4) if i or j]
    peers += [
        dev(zh_=(zh + a) % 2, zl_=(zl + b) % 4) for a in (0, 1) for b in range(4) if a or b
    ]
    loads = {}

    def load(i, name, src, dst):
        loads[name] = pltpu.make_async_copy(src, dst, isem.at[i])
        loads[name].start()

    load(0, "tok", tok_hbm, tok_ref)
    load(1, "gain", gain_hbm, gain_ref)
    load(2, "wkv", wkv_hbm, wkv_ref)
    barrier = pltpu.get_barrier_semaphore()
    for peer in peers:
        pl.semaphore_signal(barrier, inc=1, device_id=peer, device_id_type=pl.DeviceIdType.MESH)

    loads["tok"].wait()
    loads["gain"].wait()
    load(3, "wq", wq_hbm, wq_ref)
    load(4, "cot", cot_hbm, cot_ref)
    load(5, "wo", wo_hbm, wo_ref)
    load(6, "len", len_hbm, len_ref)
    gain = gain_ref[...].reshape(1, D)
    xf = tok_ref[...].astype(F32)
    rs = lax.rsqrt(jnp.mean(xf * xf, axis=-1, keepdims=True) + EPS)
    rscale[...] = rs
    nf = xf * rs * gain
    nb = nf.astype(BF16)
    normed[...] = nb
    loads["wkv"].wait()
    kvt[0, :, 0:ROWS] = mm(wkv_ref[...], nb, NT).astype(BF16)
    pl.semaphore_wait(barrier, len(peers))

    agz, agy, agr = {}, {}, {}
    lane = [slice(ROWS * d, ROWS * (d + 1)) for d in range(4)]

    parts = (slice(0, HK), slice(HK, KV))

    def to_y(d, p):
        for j in (1, 3):
            agy[j, d, p] = send(
                ("agy", j, d, p), kvt.at[0, parts[p], lane[d]], kvt.at[j, parts[p], lane[d]], dev(y_=ys[j])
            )

    def to_z(d):
        for p in (0, 1):
            agz[d, p] = send(
                ("agz", d, p), kvt.at[0, parts[p], lane[0]], kvt.at[0, parts[p], lane[d]], dev(zl_=(zl + 4 - d) % 4)
            )

    def relay_y(d):
        j, to = ((1, 3), (1, 3), (3, 1), (3, 1))[d]
        for p in (0, 1):
            agy[j, d, p].wait_recv()
            agr[d, p] = send(
                ("agr", d, p), kvt.at[j, parts[p], lane[d]], kvt.at[2, parts[p], lane[d]], dev(y_=ys[to])
            )

    def wait_z(d):
        for p in (0, 1):
            agz[d, p].wait_recv()
            to_y(d, p)

    to_z(1)
    to_z(3)
    to_y(0, 0)
    to_y(0, 1)
    to_z(2)
    loads["wq"].wait()
    q = mm(normed[...], wq_ref[...])
    for h in range(HEADS):
        qt[:, lane[h]] = q[:, lane[h]].T.astype(BF16)
    relay_y(0)
    loads["cot"].wait()
    loads["wo"].wait()
    for h in range(HEADS):
        da = mm(wo_ref[HV * h : HV * (h + 1), :], cot_ref[...], NT)
        dat[:, lane[h]] = da.astype(BF16)
    sib = dev(c_=other)
    nall[...] = normed[...].T.reshape(4, 2, 2, 96, ROWS)
    sib_n = send(("sib", "n"), nall.at[:, :, other], n2.at[:, :, :, ROWS : 2 * ROWS], sib)
    n2[:, :, :, 0:ROWS] = nall[:, :, c]
    call[...] = cot_ref[...].T.reshape(4, 2, 2, 96, ROWS)
    sib_c = send(("sib", "c"), call.at[:, :, other], c2.at[:, :, :, ROWS : 2 * ROWS], sib)
    c2[:, :, :, 0:ROWS] = call[:, :, c]
    wait_z(1)
    wait_z(3)

    x1, x3 = dev(x_=xs[1]), dev(x_=xs[3])
    xd, xf, xn = {}, {}, {}

    def to_x(w, rows, rows4):
        for h, near, to in ((0, 1, x1), (1, 3, x3)):
            for b, i in ((0, near), (1, 2)):
                xn[w, h, b] = send(("xn", w, h, b), rows.at[xs[i], h], rows4.at[h, b], to)

    sib_n.wait_recv()
    to_x(1, n2, n4)
    sib_c.wait_recv()
    to_x(0, c2, c4)
    wait_z(2)

    loads["len"].wait()
    length = len_ref[0]
    tops = [None]

    def score(j, d):
        first = (ys[j] * 4 + (zl + d) % 4) * ROWS
        blk = kvt[j, :, lane[d]]
        k = blk[0:HK, :].T
        vals[j, lane[d], :] = blk[HK:KV, :].T
        s = mm(k, qt[...]) * (SCALE * LOG2E)
        pos = first + lax.broadcasted_iota(jnp.int32, (ROWS, ALL), 0)
        s = jnp.where(pos < length, s, -1e30)
        scores[j, lane[d], :] = s
        part = jnp.max(s.reshape(ROWS // 8, 8, ALL), axis=0)
        tops[0] = part if tops[0] is None else jnp.maximum(tops[0], part)

    score(0, 0)
    score(0, 1)
    relay_y(1)
    score(0, 3)
    score(0, 2)
    relay_y(3)
    relay_y(2)
    for d, j in ((0, 1), (1, 1), (2, 3), (3, 3)):
        score(j, d)
    for j, d in ((3, 0), (3, 1), (1, 3), (1, 2)):
        for p in (0, 1):
            agy[j, d, p].wait_recv()
        score(j, d)
    for d in (0, 1, 3, 2):
        for p in (0, 1):
            agr[d, p].wait_recv()
        score(2, d)

    top = jnp.max(tops[0], axis=0, keepdims=True)
    total = jnp.zeros((8, ALL), F32)
    att = jnp.zeros((HV, ALL), F32)
    for j in range(4):
        for d in range(4):
            e = jnp.exp2(scores[j, lane[d], :] - top)
            total = total + jnp.sum(e.reshape(ROWS // 8, 8, ALL), axis=0)
            probs[j, lane[d], :] = e.astype(BF16)
        att = att + mm(kvt[j, HK:KV, :], probs[j])
    inv = 1.0 / jnp.sum(total, axis=0, keepdims=True)
    att_b = (att * inv).astype(BF16)
    da = dat[...].astype(F32)
    delta = jnp.sum(da * att_b.astype(F32), axis=0, keepdims=True)
    dats[...] = (da * inv).astype(BF16)
    qts[...] = (qt[...].astype(F32) * (inv * SCALE)).astype(BF16)
    for h in range(HEADS):
        a2[HV * h : HV * (h + 1), 0:ROWS] = att_b[:, lane[h]]
    mine, theirs = slice(0, ROWS), slice(ROWS, 2 * ROWS)
    def share(w, right, right4):
        for h, to in ((0, x1), (1, x3)):
            xd[w, h] = send(("xd", w, h), right.at[:, mine], right4.at[h, :, mine], to)

    def share_on(w, right4):
        for h in (0, 1):
            xd[w, h].wait_recv()
            xf[w, h] = send(("xf", w, h), right4.at[h, :, mine], right4.at[h, :, theirs], sib)

    sib_a = send(("sib", "a"), a2.at[:, mine], a2.at[:, theirs], sib)
    share(0, a2, a4)

    def backward(j, dq):
        for d in range(4):
            dpv = mm(vals[j, lane[d], :], dat[...])
            u = probs[j, lane[d], :].astype(F32) * (dpv - delta)
            ub[j, lane[d], :] = u.astype(BF16)
        dq = dq + mm(kvt[j, 0:HK, :], ub[j])
        t[j, 0:HK, :] = mm(qts[...], ub[j], NT).astype(BF16)
        t[j, HK:KV, :] = mm(dats[...], probs[j], NT).astype(BF16)
        return dq

    rs1, rs2, rsz = {}, {}, {}
    hop1, hop2 = (1, 1, 3, 3), (3, 3, 1, 1)

    def rs_opp(d):
        rs1[d, 1] = send(("rs1", d, 1), t.at[2, :, lane[d]], r1.at[d, 1], dev(y_=ys[hop1[d]]))

    def rs_own(d):
        rs1[d, 0] = send(("rs1", d, 0), t.at[hop1[d], :, lane[d]], r1.at[d, 0], dev(y_=ys[hop1[d]]))

    def rs_fwd(d):
        rs1[d, 1].wait_recv()
        f[d] = (t[hop2[d], :, lane[d]].astype(F32) + r1[d, 1].astype(F32)).astype(BF16)
        rs2[d] = send(("rs2", d), f.at[d], r2.at[d], dev(y_=ys[hop2[d]]))

    def rs_sum(d):
        rs1[d, 0].wait_recv()
        rs2[d].wait_recv()
        total = t[0, :, lane[d]].astype(F32) + r1[d, 0].astype(F32) + r2[d].astype(F32)
        zsend[d] = total.astype(BF16)
        if d:
            rsz[d] = send(("rsz", d), zsend.at[d], rz.at[d - 1], dev(zl_=(zl + d) % 4))

    po, pf, sx = (po0, po1), (pf0, pf1), (sx0, sx1)
    yb, ry, ysum = (y0, y1), (ry0, ry1), (ys0, ys1, ys2)
    zb, rzb = (z0, z1, z2), (rz0, rz1, rz2)
    grads, grads_hbm = (gwo_ref, gwq_ref, gwkv_ref), (gwo_hbm, gwq_hbm, gwkv_hbm)
    wx2, wy, wz = {}, {}, {}

    def w_part(w, rows, rows4, right, right4):
        for h, far, to in ((0, 3, x3), (1, 1, x1)):
            left = jnp.concatenate([rows[xs[far], h], rows[x, h]], axis=0)
            xn[w, h, 0].wait_recv()
            xn[w, h, 1].wait_recv()
            left4 = jnp.concatenate([rows4[h, 1], rows4[h, 0]], axis=0)
            xf[w, h].wait_recv()
            both = mm(left, right[...], NT) + mm(left4, right4[h], NT)
            pf[w][h] = both[0:96].astype(BF16)
            wx2[w, h] = send(("wx2", w, h), pf[w].at[h], sx[w].at[h], to)
            po[w][h] = both[96:192]

    def w_y(w):
        sums = []
        for h in (0, 1):
            wx2[w, h].wait_recv()
            sums.append(po[w][h] + sx[w][h].astype(F32))
        for k in range(4):
            rows = slice(24 * k, 24 * (k + 1))
            yb[w][k] = jnp.concatenate([sums[0][rows], sums[1][rows]], axis=0).astype(BF16)
        for j in (2, 1, 3):
            wy[w, j] = send(("wy", w, j), yb[w].at[ys[j]], ry[w].at[j - 1], dev(y_=ys[j]))

    wxy = {}

    def kv_part():
        for i in (2, 1, 3, 0):
            left = n2[xs[i]].reshape(192, 2 * ROWS)
            rows = mm(left, dkv2[...], NT)
            for k in range(4):
                piece = [rows[96 * h + 24 * k : 96 * h + 24 * (k + 1)] for h in (0, 1)]
                pk[i, k] = jnp.concatenate(piece, axis=0).astype(BF16)
            for j in (2, 1, 3, 0):
                if i or j:
                    wxy[i, j] = send(
                        ("wxy", i, j), pk.at[i, ys[j]], rk.at[4 * i + j], dev(x_=xs[i], y_=ys[j])
                    )

    def w_z(w):
        if w == 2:
            total = pk[0, y].astype(F32)
            for i in (0, 1, 3, 2):
                for j in (0, 1, 3, 2):
                    if i or j:
                        wxy[i, j].wait_recv()
                        total = total + rk[4 * i + j].astype(F32)
        else:
            total = yb[w][y].astype(F32)
            for j in (1, 3, 2):
                wy[w, j].wait_recv()
                total = total + ry[w][j - 1].astype(F32)
        ysum[w][0:48, :] = total
        ysum[w][48:56, :] = jnp.zeros((8, COLS[w]), F32)
        for k in range(8):
            rows = ysum[w][6 * k : 6 * k + 8, :]
            right = rows[:, HALF[w] :]
            if right.shape[1] < HALF[w]:
                right = jnp.concatenate([right, jnp.zeros((8, HALF[w] - right.shape[1]), F32)], axis=1)
            zb[w][k] = jnp.concatenate([rows[:, : HALF[w]], right], axis=0).astype(BF16)
        for a, b in ((1, 0), (1, 1), (1, 3), (1, 2), (0, 2), (0, 1), (0, 3)):
            zh_, zl_ = (zh + a) % 2, (zl + b) % 4
            wz[w, a, b] = send(
                ("wz", w, a, b), zb[w].at[zh_ * 4 + zl_], rzb[w].at[a * 4 + b - 1], dev(zh_=zh_, zl_=zl_)
            )

    def w_end(w):
        total = zb[w][zh * 4 + zl].astype(F32)
        for a, b in ((0, 1), (0, 3), (0, 2), (1, 0), (1, 1), (1, 3), (1, 2)):
            wz[w, a, b].wait_recv()
            total = total + rzb[w][a * 4 + b - 1].astype(F32)
        grads[w][:, : HALF[w]] = total[0:6]
        grads[w][:, HALF[w] :] = total[8:14, : COLS[w] - HALF[w]]

    dq = backward(2, jnp.zeros((HK, ALL), F32))
    for d in (1, 2, 0, 3):
        rs_opp(d)
    dq = backward(1, dq)
    rs_own(1)
    dq = backward(3, dq)
    rs_own(2)
    dq = backward(0, dq)
    dq_b = (dq * (inv * SCALE)).astype(BF16)
    for h in range(HEADS):
        dq2[HK * h : HK * (h + 1), mine] = dq_b[:, lane[h]]
    sib_q = send(("sib", "q"), dq2.at[:, mine], dq2.at[:, theirs], sib)
    share(1, dq2, dq4)
    rs_fwd(1)
    rs_fwd(2)
    rs_own(0)
    rs_own(3)
    share_on(0, a4)
    rs_fwd(0)
    rs_fwd(3)
    sib_a.wait_recv()
    w_part(0, c2, c4, a2, a4)
    rs_sum(1)
    rs_sum(2)
    share_on(1, dq4)
    sib_q.wait_recv()
    w_part(1, n2, n4, dq2, dq4)
    rs_sum(3)
    rs_sum(0)
    dqn = jnp.concatenate([dq2[HK * h : HK * (h + 1), mine].T for h in range(HEADS)], axis=1)
    dn[...] = mm(dqn, wq_ref[...], NT)
    w_y(0)
    dkv = zsend[0].astype(F32)
    for d in (1, 2, 3):
        rsz[d].wait_recv()
        dkv = dkv + rz[d - 1].astype(F32)
    dkv_b = dkv.astype(BF16)
    dkv2[:, mine] = dkv_b
    sib_kv = send(("sib", "kv"), dkv2.at[:, mine], dkv2.at[:, theirs], sib)
    dkvn = jnp.concatenate([dkv_b[0:HK].T, dkv_b[HK:KV].T], axis=1)
    dn[...] += mm(dkvn, wkv_ref[...])
    w_y(1)
    sib_kv.wait_recv()
    kv_part()
    w_z(0)
    w_z(1)
    xf = tok_ref[...].astype(F32)
    rs = rscale[...]
    gd = gain_ref[...].reshape(1, D) * dn[...]
    inner = jnp.mean(xf * gd, axis=-1, keepdims=True)
    out = cot_ref[...].astype(F32) + rs * gd - xf * (rs * rs * rs * inner)
    gtok_ref[...] = out.astype(BF16)
    stores = [pltpu.make_async_copy(gtok_ref, gtok_hbm, osem.at[3])]
    stores[0].start()
    w_z(2)
    for w in range(3):
        w_end(w)
        stores.append(pltpu.make_async_copy(grads[w], grads_hbm[w], osem.at[w]))
        stores[-1].start()
    for copy in sent:
        copy.wait_send()
    for copy in stores:
        copy.wait()


def hand_on(*refs):
    come, go = refs[12], refs[13]
    first = [pltpu.make_async_copy(refs[i], refs[8 + i], come.at[i]) for i in range(4)]
    second = [pltpu.make_async_copy(refs[8 + i], refs[4 + i], go.at[i]) for i in range(4)]
    for copy in first:
        copy.start()
    for i in range(4):
        first[i].wait()
        second[i].start()
    for copy in second:
        copy.wait()


def body(tokens, lengths, cotangent, gain, w_q, w_kv, w_o):
    hbm = pl.BlockSpec(memory_space=pltpu.HBM)

    def per_weight(shape, kind):
        return [pltpu.VMEM(shape(n), kind) for n in COLS]

    scratch = [
        pltpu.SMEM((1,), jnp.int32),
        pltpu.VMEM((ROWS, D), BF16),
        pltpu.VMEM((ROWS, D), BF16),
        pltpu.VMEM((D,), F32),
        pltpu.VMEM((D, COLS[1]), BF16),
        pltpu.VMEM((KV, D), BF16),
        pltpu.VMEM((HEADS * HV, D), BF16),
        pltpu.VMEM((ROWS, D), BF16),
        pltpu.VMEM((6, COLS[1]), F32),
        pltpu.VMEM((6, COLS[2]), F32),
        pltpu.VMEM((6, COLS[0]), F32),
        pltpu.VMEM((4, KV, CHUNK), BF16),
        pltpu.VMEM((4, CHUNK, HV), BF16),
        pltpu.VMEM((4, CHUNK, ALL), F32),
        pltpu.VMEM((4, CHUNK, ALL), BF16),
        pltpu.VMEM((4, CHUNK, ALL), BF16),
        pltpu.VMEM((HK, ALL), BF16),
        pltpu.VMEM((HK, ALL), BF16),
        pltpu.VMEM((HV, ALL), BF16),
        pltpu.VMEM((HV, ALL), BF16),
        pltpu.VMEM((ROWS, D), BF16),
        pltpu.VMEM((ROWS, 1), F32),
        pltpu.VMEM((ROWS, D), F32),
        pltpu.VMEM((4, KV, CHUNK), BF16),
        pltpu.VMEM((4, 2, KV, ROWS), BF16),
        pltpu.VMEM((4, KV, ROWS), BF16),
        pltpu.VMEM((4, KV, ROWS), BF16),
        pltpu.VMEM((4, KV, ROWS), BF16),
        pltpu.VMEM((3, KV, ROWS), BF16),
        pltpu.VMEM((4, 2, 2, 96, ROWS), BF16),
        pltpu.VMEM((4, 2, 2, 96, ROWS), BF16),
        pltpu.VMEM((4, 2, 96, 2 * ROWS), BF16),
        pltpu.VMEM((4, 2, 96, 2 * ROWS), BF16),
        pltpu.VMEM((COLS[0], 2 * ROWS), BF16),
        pltpu.VMEM((COLS[1], 2 * ROWS), BF16),
        pltpu.VMEM((COLS[2], 2 * ROWS), BF16),
    ]
    scratch += [pltpu.VMEM((2, 2, 96, 2 * ROWS), BF16)] * 2
    scratch += per_weight(lambda n: (2, n, 2 * ROWS), BF16)[:2]
    scratch += per_weight(lambda n: (2, 96, n), F32)[:2]
    scratch += per_weight(lambda n: (2, 96, n), BF16)[:2]
    scratch += per_weight(lambda n: (2, 96, n), BF16)[:2]
    scratch += per_weight(lambda n: (4, 48, n), BF16)[:2]
    scratch += per_weight(lambda n: (3, 48, n), BF16)[:2]
    scratch += [pltpu.VMEM((4, 4, 48, KV), BF16), pltpu.VMEM((16, 48, KV), BF16)]
    scratch += per_weight(lambda n: (56, n), F32)
    scratch += [pltpu.VMEM((8, 16, n), BF16) for n in HALF]
    scratch += [pltpu.VMEM((7, 16, n), BF16) for n in HALF]
    scratch += [pltpu.SemaphoreType.DMA((len(SLOT),)), pltpu.SemaphoreType.DMA((len(SLOT),))]
    scratch += [pltpu.SemaphoreType.DMA((7,)), pltpu.SemaphoreType.DMA((4,))]
    results = (
        jax.ShapeDtypeStruct((ROWS, D), BF16),
        jax.ShapeDtypeStruct((6, COLS[1]), F32),
        jax.ShapeDtypeStruct((6, COLS[2]), F32),
        jax.ShapeDtypeStruct((6, COLS[0]), F32),
    )
    outs = pl.pallas_call(
        kernel,
        out_shape=results,
        in_specs=[hbm] * 7,
        out_specs=(hbm,) * 4,
        scratch_shapes=scratch,
        compiler_params=pltpu.CompilerParams(
            collective_id=0, has_side_effects=True, vmem_limit_bytes=56 * 1024 * 1024
        ),
    )(lengths, tokens[0], cotangent[0], gain, w_q, w_kv.T, w_o)
    grad_x, grad_wq, grad_wkv, grad_wo_t = pl.pallas_call(
        hand_on,
        out_shape=results,
        in_specs=[hbm] * 4,
        out_specs=(hbm,) * 4,
        scratch_shapes=[pltpu.VMEM(r.shape, r.dtype) for r in results]
        + [pltpu.SemaphoreType.DMA((4,)), pltpu.SemaphoreType.DMA((4,))],
        compiler_params=pltpu.CompilerParams(vmem_limit_bytes=60 * 1024 * 1024),
    )(*outs)
    return grad_x[None], grad_wq, grad_wkv, grad_wo_t


def solution(mesh):
    return jax.shard_map(
        body,
        mesh=mesh,
        in_specs=(P("dp", "seq", None), P("dp"), P("dp", "seq", None), P(), P(), P(), P()),
        out_specs=(
            P("dp", "seq", None),
            P(("dp", "seq"), None),
            P(("dp", "seq"), None),
            P(("dp", "seq"), None),
        ),
        check_vma=False,
    )
```
